128 devices in a mesh: gx: 8 (over z_hi, y), gy: 16 (over x, z_lo, core).
Axes of the slice: x: 4, y: 4, z: 4 (z_hi: 2, z_lo: 2; z = z_hi * 2 + z_lo), core: 2. Of those that a mesh axis runs over, the one named last changes fastest.
Arguments:
- wave_now: float32 [3, 32, 256, 2048], P(None, None, 'gx', 'gy'), may hold values from -5 to 5, as said below
- wave_prev: float32 [3, 32, 256, 2048], P(None, None, 'gx', 'gy'), may hold values from -6 to 6
- shear_mod: float32 [32, 256, 2048], P(None, 'gx', 'gy'), may hold values from 0.02 to 0.06
- bulk_mod: float32 [32, 256, 2048], P(None, 'gx', 'gy'), may hold values from 0.02 to 0.08
- found_cell: int32 [8, 16, 128, 4], P('gx', 'gy'), may hold values from 0 to 4095
- support_row: int32 [2, 16384], P(None, ('gx', 'gy')), may hold values from 0 to 511, as said below
- block_col: int32 [16, 4, 16384], P(None, None, ('gx', 'gy')), may hold values from 0 to 15, as said below
- block_val: float32 [16, 4, 6, 6, 16384], P(None, None, None, None, ('gx', 'gy')), may hold values from -0.36 to 0.36
- mass_inv: float32 [16, 6, 16384], P(None, None, ('gx', 'gy')), may hold values from 0.5 to 1.5
- bridge_disp: float32 [16, 6, 16384], P(None, None, ('gx', 'gy')), may hold values from -6 to 6
- bridge_vel: float32 [16, 6, 16384], P(None, None, ('gx', 'gy')), may hold values from -6 to 6
- bridge_acc: float32 [16, 6, 16384], P(None, None, ('gx', 'gy')), may hold values from -6 to 6
Outputs:
- wave_out: float32 [3, 32, 256, 2048], P(None, None, 'gx', 'gy')
- wave_before: float32 [3, 32, 256, 2048], P(None, None, 'gx', 'gy')
- deck_disp: float32 [16, 6, 16384], P(None, None, ('gx', 'gy'))
- deck_vel: float32 [16, 6, 16384], P(None, None, ('gx', 'gy'))
The draws below stay inside these ranges and needn't reach their ends.
Inputs may be any that keep to these rules, and one draw needn't show every extreme that they name: `wave_now`: normal values clipped to the range; in other draws a broad positive part may be added. `support_row`: for each owner, the 2 x 128 entries of its bridge sections are distinct and fill all 4 slots of exactly 64 source tiles; which tiles varies by owner. `block_col`: in each block row of each section the 4 block columns are distinct and the first is the row itself.
All inputs are finite; a program needn't handle non-finite values.
Results may differ from the reference program's by a relative error of at most 0.0001.
Values sent between devices are 32-bit elements; how exact they have to be, the bound alone decides.
A program may use at most 64 MiB of HBM per device.

```python
import math
import jax
import jax.numpy as jnp
from jax import lax

CX = 32
CY = 128
NZ = 32
STEPS = 10
NODES = 16
DOFS = 6
NNZB = 4
SUPPORTS = 2
BR_DEV = 128
NX = 256
NY = 2048
BRIDGES = 16384
SLOTS = 4
SOURCES = 64
N_GX = 8
N_GY = 16
DEVICES = 128


def draw_wave_now(key, part):
    shape_all = (3, NZ, NX, NY)
    return jnp.clip(jax.random.normal(key, shape_all, jnp.float32), -5.0, 5.0)


def draw_support_row(key, part):
    owner_count = BRIDGES // BR_DEV
    row_count = BR_DEV * SUPPORTS
    weights = jax.random.randint(jax.random.fold_in(key, 1), (owner_count,), 1, 5)
    raw_scores = jax.random.randint(jax.random.fold_in(key, 2), (owner_count, owner_count), 0, 256)
    scores = raw_scores * weights[None, :] * owner_count + jnp.arange(owner_count, dtype=jnp.int32)[None, :]
    order = jnp.argsort(-scores, axis=1)
    chosen = order[:, :SOURCES]
    live_rows = (chosen[:, :, None] * SLOTS + jnp.arange(SLOTS, dtype=jnp.int32)[None, None, :]).reshape(owner_count, row_count)
    mixing = jax.random.randint(jax.random.fold_in(key, 3), (owner_count, row_count), 0, 4096) * row_count + jnp.arange(row_count, dtype=jnp.int32)[None, :]
    shuffle = jnp.argsort(mixing, axis=1)
    rows_out = jnp.take_along_axis(live_rows, shuffle, axis=1)
    rows_out = rows_out.reshape(owner_count, SUPPORTS, BR_DEV)
    rows_out = jnp.transpose(rows_out, (1, 0, 2)).reshape(SUPPORTS, BRIDGES)
    return rows_out.astype(jnp.int32)


def draw_block_col(key, part):
    raw_scores = jax.random.randint(key, (NODES, BRIDGES, NODES - 1), 0, 4096)
    scores = raw_scores * (NODES - 1) + jnp.arange(NODES - 1, dtype=jnp.int32)[None, None, :]
    offsets = jnp.argsort(scores, axis=-1)[:, :, :NNZB - 1] + 1
    row_ids = jnp.arange(NODES, dtype=jnp.int32)[:, None, None]
    others = (row_ids + offsets) % NODES
    itself = jnp.broadcast_to(row_ids, (NODES, BRIDGES, 1))
    columns = jnp.concatenate([itself, others.astype(jnp.int32)], axis=-1)
    return jnp.transpose(columns, (0, 2, 1)).astype(jnp.int32)


def set_ends(values, rng, low, top_value):
    longest = values.shape.index(max(values.shape))
    spots = []
    for shift in (0, 1):
        where = [jax.random.randint(jax.random.fold_in(rng, axis), (), 0, length) for axis, length in enumerate(values.shape)]
        where[longest] = (where[longest] + shift) % values.shape[longest]
        spots.append(tuple(where))
    return values.at[spots[0]].set(low).at[spots[1]].set(top_value)


def block_levels(rng, dims, cuts, low, high):
    def one(position, parts):
        draws = jax.random.uniform(jax.random.fold_in(jax.random.fold_in(rng, 6), position), (parts,), jnp.float32, low / len(cuts), high / len(cuts))
        return jnp.repeat(jnp.exp(draws), dims[position] // parts).reshape((-1,) + (1,) * (len(dims) - position - 1))

    factor_of = one(*cuts[0])
    for cut in cuts[1:]:
        factor_of = factor_of * one(*cut)
    return factor_of


def gaussian(key, dims, scale, most, cuts=(), kind=jnp.bfloat16):
    values = jax.random.normal(key, dims, jnp.float32) * scale
    if len(cuts) > 0:
        values = block_levels(key, dims, cuts, -0.22, 0.18) * values
    return jnp.clip(values, min=-most, max=most).astype(kind)


def setup_inputs(seed: int = 0) -> dict:
    splits = jax.random.split(jax.random.key(seed), 13)
    wave_now = draw_wave_now(jax.random.fold_in(splits[12], 71), 0)
    wave_prev = gaussian(splits[1], (3, NZ, NX, NY), 1.0, 6.0, ((2, 8), (3, 16)), jnp.float32)
    shear_mod = jnp.clip(jnp.exp(math.log(0.06) - 1.0986123 * jax.random.uniform(splits[2], (NZ, NX, NY), jnp.float32) ** block_levels(splits[2], (NZ, NX, NY), ((1, 8), (2, 16)), -0.2, 0.2)), 0.02, 0.06)
    bulk_mod = jnp.clip(jnp.exp(math.log(0.08) - 1.3862944 * jax.random.uniform(splits[3], (NZ, NX, NY), jnp.float32) ** block_levels(splits[3], (NZ, NX, NY), ((1, 8), (2, 16)), -0.2, 0.2)), 0.02, 0.08)
    found_cell = set_ends(jax.random.randint(splits[4], (N_GX, N_GY, DEVICES, SLOTS), 0, CX * CY), jax.random.fold_in(splits[4], 1), 0, (CX * CY) - 1).astype(jnp.int32)
    support_row = draw_support_row(jax.random.fold_in(splits[12], 71), 0)
    block_col = draw_block_col(jax.random.fold_in(splits[12], 71), 0)
    block_val = gaussian(splits[7], (NODES, NNZB, DOFS, DOFS, BRIDGES), 0.06, 0.36, ((4, 128),), jnp.float32)
    mass_inv = jnp.clip(jnp.exp(math.log(1.5) - 1.0986123 * jax.random.uniform(splits[8], (NODES, DOFS, BRIDGES), jnp.float32) ** block_levels(splits[8], (NODES, DOFS, BRIDGES), ((2, 128),), -0.2, 0.2)), 0.5, 1.5)
    bridge_disp = gaussian(splits[9], (NODES, DOFS, BRIDGES), 1.0, 6.0, ((2, 128),), jnp.float32)
    bridge_vel = gaussian(splits[10], (NODES, DOFS, BRIDGES), 1.0, 6.0, ((2, 128),), jnp.float32)
    bridge_acc = gaussian(splits[11], (NODES, DOFS, BRIDGES), 1.0, 6.0, ((2, 128),), jnp.float32)
    return dict(wave_now=wave_now, wave_prev=wave_prev, shear_mod=shear_mod, bulk_mod=bulk_mod, found_cell=found_cell, support_row=support_row, block_col=block_col, block_val=block_val, mass_inv=mass_inv, bridge_disp=bridge_disp, bridge_vel=bridge_vel, bridge_acc=bridge_acc)


def first_diff(padded, which_axis):
    length = padded.shape[which_axis] - 4
    pieces = [lax.slice_in_dim(padded, offset, offset + length, axis=which_axis) for offset in range(5)]
    return (pieces[0] - 8.0 * pieces[1] + 8.0 * pieces[3] - pieces[4]) / 12.0


def second_diff(padded, which_axis):
    length = padded.shape[which_axis] - 4
    pieces = [lax.slice_in_dim(padded, offset, offset + length, axis=which_axis) for offset in range(5)]
    return (-pieces[0] + 16.0 * pieces[1] - 30.0 * pieces[2] + 16.0 * pieces[3] - pieces[4]) / 12.0


def trim_rest(values, inner_shape):
    for which_axis in range(3):
        if values.shape[which_axis] != inner_shape[which_axis]:
            values = lax.slice_in_dim(values, 2, 2 + inner_shape[which_axis], axis=which_axis)
    return values


def wave_accel(padded, shear_mod, bulk_mod):
    inner_shape = shear_mod.shape
    axis_of = (1, 2, 0)
    slopes = [first_diff(padded[component], axis_of[component]) for component in range(3)]
    result = []
    for component in range(3):
        curves = [trim_rest(second_diff(padded[component], which_axis), inner_shape) for which_axis in range(3)]
        laplace = curves[0] + curves[1] + curves[2]
        diverge = curves[axis_of[component]]
        for second in range(3):
            if second != component:
                diverge = diverge + trim_rest(first_diff(slopes[second], axis_of[component]), inner_shape)
        result.append(shear_mod * laplace + bulk_mod * diverge)
    return jnp.stack(result)


def stiff_apply(displace, block_val, block_col):
    flipped = jnp.transpose(displace, (2, 0, 1))
    number = jnp.arange(displace.shape[2], dtype=jnp.int32)
    picked = flipped[number[None, None, :], block_col]
    picked = jnp.transpose(picked, (0, 1, 3, 2))
    return displace + jnp.sum(block_val * picked[:, :, None, :, :], axis=(1, 3))


def bridge_advance(displace, velocity, accelerate, ground, mass_inv, block_val, block_col):
    new_disp = displace + velocity + 0.5 * accelerate
    node_count = displace.shape[0]
    forcing = jnp.zeros_like(displace)
    forcing = forcing.at[0, 0:3].set(ground[:, 0])
    forcing = forcing.at[node_count - 1, 0:3].set(ground[:, 1])
    new_acc = mass_inv * (forcing - stiff_apply(new_disp, block_val, block_col))
    new_vel = velocity + 0.5 * (accelerate + new_acc)
    return new_disp, new_vel, new_acc


def reference(wave_now, wave_prev, shear_mod, bulk_mod, found_cell, support_row, block_col, block_val, mass_inv, bridge_disp, bridge_vel, bridge_acc):
    owners = jnp.arange(BRIDGES, dtype=jnp.int32) // BR_DEV
    source = support_row // SLOTS
    slot_at = support_row % SLOTS
    src_x = source // N_GY
    src_y = source % N_GY
    local_cell = found_cell[src_x, src_y, owners[None, :], slot_at]
    east_cell = src_x * CX + local_cell // CY
    north_cell = src_y * CY + local_cell % CY
    current = wave_now
    previous = wave_prev
    displace, velocity, accelerate = bridge_disp, bridge_vel, bridge_acc
    for substep in range(STEPS):
        padded = jnp.pad(current, ((0, 0), (2, 2), (2, 2), (2, 2)))
        following = 2.0 * current - previous + wave_accel(padded, shear_mod, bulk_mod)
        previous = current
        current = following
        ground = current[:, 0][:, east_cell, north_cell]
        displace, velocity, accelerate = bridge_advance(displace, velocity, accelerate, ground, mass_inv, block_val, block_col)
    return current, previous, displace, velocity
```

```python
import functools

import jax
import jax.numpy as jnp
import ml_dtypes
import numpy as np
from jax import lax
from jax.experimental import pallas as pl
from jax.experimental.pallas import tpu as pltpu
from jax.sharding import PartitionSpec as P

MESH = pl.DeviceIdType.MESH
F32, BF = jnp.float32, jnp.bfloat16
STEPS = 10
GX, GY = 8, 16
R = 144
GR = 4
VMEM = pltpu.VMEM


def band(coefs, delta):
    k, n = np.arange(128)[:, None], np.arange(128)[None, :]
    dx = (k // 32 + 4 * delta) - n // 32
    dz = k % 32 - n % 32
    out = np.zeros((128, 128), np.float32)
    for (a, b), v in coefs.items():
        out[(dx == a) & (dz == b)] = v
    return out


def band_weights():
    c1 = {-2: 1, -1: -8, 1: 8, 2: -1}
    c2 = {-2: -1, -1: 16, 0: -30, 1: 16, 2: -1}
    dx = {(a, 0): v for a, v in c1.items()}
    dz = {(0, a): v for a, v in c1.items()}
    dxx = {(a, 0): v for a, v in c2.items()}
    dzz = {(0, a): v for a, v in c2.items()}
    dxz = {(a, b): v * w for a, v in c1.items() for b, w in c1.items()}
    lap = dict(dxx)
    for key, v in dzz.items():
        lap[key] = lap.get(key, 0) + v
    dxx12 = {key: 12 * v for key, v in dxx.items()}
    dzz12 = {key: 12 * v for key, v in dzz.items()}

    def two(m):
        return np.concatenate([m, m], 0)

    def beside(o):
        return np.where(np.arange(128)[:, None] < 64, band(o, 1), band(o, -1))

    def inner(ops):
        return np.concatenate([two(band(o, 0)) for o in ops], 1)

    def full(ops):
        return np.concatenate([inner(ops), np.concatenate([two(beside(o)) for o in ops], 1)], 0)

    def select(c):
        k, n = np.arange(128)[:, None], np.arange(128)[None, :]
        return two(((k % 32 == 0) & (n % 12 == c * 4 + k // 32) & (n < 120)).astype(np.float32))

    wu = full([lap, dxx12, dxz, dx])
    ww = full([lap, dxz])
    ww0 = inner([dzz12, dz])
    wv = full([lap, dx])
    wv0 = np.concatenate([inner([dz]), select(1)], 1)
    wsel = np.stack([select(0), select(2)])
    return [jnp.asarray(a.astype(ml_dtypes.bfloat16)) for a in (wu, ww, ww0, wv, wv0, wsel)]


def d1(m2, m1, p1, p2):
    return (m2 - p2) + 8.0 * (p1 - m1)


def wave_kernel(
    now, prev, shear, bulk, found, wu, ww, ww0, wv, wv0, wsel,
    out_now, out_prev, out_ground,
    WA, WB, SB, BH, MU, HU, HIST, PS, PR, send_sem, recv_sem,
):
    gx, gy = lax.axis_index("gx"), lax.axis_index("gy")

    def has(dx, dy):
        return (gx + dx >= 0) & (gx + dx < GX) & (gy + dy >= 0) & (gy + dy < GY)

    dirs = [(1, 0), (-1, 0), (0, 1), (0, -1), (1, 1), (1, -1), (-1, 1), (-1, -1)]
    WS = (WA, WB)
    lane = lax.broadcasted_iota(jnp.int32, (64, 128), 1)

    for W in WS:
        W[...] = jnp.zeros_like(W)
    PR[...] = jnp.zeros_like(PR)
    BH[...] = jnp.zeros_like(BH)
    HIST[...] = jnp.zeros_like(HIST)

    barrier = pltpu.get_barrier_semaphore()
    count = 0
    for dx, dy in dirs:
        ok = has(dx, dy)
        count = count + ok.astype(jnp.int32)

        @pl.when(ok)
        def _():
            pl.semaphore_signal(barrier, inc=1, device_id={"gx": gx + dx, "gy": gy + dy}, device_id_type=MESH)

    for c in range(3):
        for src, W in ((now, WA), (prev, WB)):

            def load_field(xs, _):
                rows = [src[c, pl.ds(xs * 4 + xl + 256 * q, 8, stride=32), :] for xl in range(4) for q in range(4)]
                W[c, xs + 1, 8:136, :] = jnp.concatenate(rows, 0).T
                return 0

            lax.fori_loop(0, 8, load_field, 0)
    for i, src in enumerate((shear, bulk)):

        def load_mod(xs, _):
            rows = [src[pl.ds(xs * 4 + xl + 256 * q, 8, stride=32), :] for xl in range(4) for q in range(4)]
            SB[i, xs] = jnp.concatenate(rows, 0).T * (1.0 / 12.0 if i == 0 else 1.0 / 144.0)
            return 0

        lax.fori_loop(0, 8, load_mod, 0)

    pl.semaphore_wait(barrier, count)

    def copy(p, d):
        dx, dy = dirs[d]
        W = WS[p]
        if dy == 0:
            side = 1 if dx > 0 else 0
            src, dst = PS.at[p, side], PR.at[p, 1 - side]
        else:
            y_src, y_dst = (134, 6) if dy > 0 else (8, 136)
            if dx == 0:
                src, dst = W.at[:, 1:9, pl.ds(y_src, 2), :], W.at[:, 1:9, pl.ds(y_dst, 2), :]
            else:
                x_src, x_dst = (8, 0) if dx > 0 else (1, 9)
                src, dst = W.at[0:2, x_src, pl.ds(y_src, 2), :], W.at[0:2, x_dst, pl.ds(y_dst, 2), :]
        return pltpu.make_async_remote_copy(
            src_ref=src, dst_ref=dst, send_sem=send_sem.at[p, d], recv_sem=recv_sem.at[p, d],
            device_id={"gx": gx + dx, "gy": gy + dy}, device_id_type=MESH,
        )

    def send(p):
        W = WS[p]
        for c in range(3):
            low, high = W[c, 8, 8:72, :], W[c, 8, 72:136, :]
            PS[p, 1, c] = jnp.where(lane < 64, pltpu.roll(low, 64, 1), high)
            low, high = W[c, 1, 8:72, :], W[c, 1, 72:136, :]
            PS[p, 0, c] = jnp.where(lane < 64, low, pltpu.roll(high, 64, 1))
        for d, (dx, dy) in enumerate(dirs):

            @pl.when(has(dx, dy))
            def _():
                copy(p, d).start()

    def finish(p):
        for d, (dx, dy) in enumerate(dirs):

            @pl.when(has(-dx, -dy))
            def _():
                copy(p, d).wait_recv()

        for d, (dx, dy) in enumerate(dirs):

            @pl.when(has(dx, dy))
            def _():
                copy(p, d).wait_send()

        W = WS[p]
        for c in range(3):
            left, right = PR[p, 0, c], PR[p, 1, c]
            W[c, 0, 8:72, :] = pltpu.roll(left, 64, 1)
            W[c, 0, 72:136, :] = left
            W[c, 9, 8:72, :] = right
            W[c, 9, 72:136, :] = pltpu.roll(right, 64, 1)

    def split_slab(W, c, xs, own=True, up=True, down=True):
        x = W[c, xs]
        hi = x.astype(BF)
        lo = (x - hi.astype(F32)).astype(BF)
        at = xs * R if isinstance(xs, int) else pl.multiple_of(xs * R, R)
        if own:
            BH[c, pl.ds(at, R), 0:128] = hi
            BH[c, pl.ds(at, R), 128:256] = lo
        if up:
            BH[c, pl.ds(at + R, R), 320:384] = hi[:, 64:128]
            BH[c, pl.ds(at + R, R), 448:512] = lo[:, 64:128]
        if down:
            BH[c, pl.ds(at - R, R), 256:320] = hi[:, 0:64]
            BH[c, pl.ds(at - R, R), 384:448] = lo[:, 0:64]

    def split_all(W):
        def body(xs, _):
            for c in range(3):
                split_slab(W, c, xs + 1)
            return 0

        lax.fori_loop(0, 8, body, 0)
        for c in range(3):
            split_slab(W, c, 0, own=False, down=False)
            split_slab(W, c, 9, own=False, up=False)

    dot = functools.partial(jnp.dot, preferred_element_type=F32)
    n = GR * R

    def matmuls(g):
        at = pl.multiple_of(g * n + R, R)
        u = dot(BH[0, pl.ds(at, n), :], wu[...])
        w = dot(BH[2, pl.ds(at, n), :], ww[...])
        w0 = dot(BH[2, pl.ds(at, n), 0:256], ww0[...])
        v = dot(BH[1, pl.ds(at, n), :], wv[...])
        v0 = dot(BH[1, pl.ds(at, n), 0:256], wv0[...])
        part = lambda a: a.reshape(GR, R, 128)
        MU[0] = part(u[:, 0:128])
        MU[1] = part(v[:, 0:128])
        MU[2] = part(w[:, 0:128])
        MU[3] = part(u[:, 128:256] + w[:, 128:256])
        MU[4] = part(u[:, 256:384] + w0[:, 0:128])
        MU[5] = part(u[:, 384:512] + w0[:, 128:256])
        MU[6] = part(v[:, 128:256])
        MU[7] = part(v0[:, 0:128])
        return v0[:, 128:256]

    def surface(g, picked, t):
        at = pl.multiple_of(g * n + R, R)
        picked = picked + dot(BH[0, pl.ds(at, n), 0:256], wsel[0]) + dot(BH[2, pl.ds(at, n), 0:256], wsel[1])
        group = lax.broadcasted_iota(jnp.int32, (GR, 128, 128), 2) // 12
        where = pl.ds(g * GR, GR)
        HIST[where] = jnp.where(group == t, picked.reshape(GR, R, 128)[:, 8:136, :], HIST[where])

    def update(g, j, W, N):
        xs = g * GR + j
        D = (-2, -1, 1, 2)
        for yb in range(16):
            r = lambda d: pl.ds(8 + yb * 8 + d, 8)
            sh = SB[0, xs, yb * 8 : yb * 8 + 8, :]
            bu = SB[1, xs, yb * 8 : yb * 8 + 8, :]
            mix = [
                MU[3, j, r(0), :] + d1(*[MU[6, j, r(d), :] for d in D]),
                d1(*[MU[5, j, r(d), :] for d in D]),
                MU[4, j, r(0), :] + d1(*[MU[7, j, r(d), :] for d in D]),
            ]
            for c in range(3):
                y = [W[c, xs + 1, r(d), :] for d in D]
                mid = W[c, xs + 1, r(0), :]
                dyy = 16.0 * (y[1] + y[2]) - (y[0] + y[3]) - 30.0 * mid
                lap = MU[c, j, r(0), :] + dyy
                b = mix[c] + 12.0 * dyy if c == 1 else mix[c]
                N[c, xs + 1, r(0), :] = (2.0 * mid - N[c, xs + 1, r(0), :]) + (sh * lap + bu * b)

    def substep(p, t):
        W, N = WS[p], WS[1 - p]
        finish(p)
        split_all(W)

        def body(g, _):
            picked = matmuls(g)
            surface(g, picked, t)
            for j in range(GR):
                update(g, j, W, N)
            return 0

        lax.fori_loop(0, 8 // GR, body, 0)

    send(0)

    def pair(i, _):
        substep(0, 2 * i - 1)
        send(1)
        substep(1, 2 * i)

        @pl.when(i < STEPS // 2 - 1)
        def _():
            send(0)

        return 0

    lax.fori_loop(0, STEPS // 2, pair, 0)

    def last(xs, _):
        for c in range(3):
            split_slab(WA, c, xs + 1, up=False, down=False)
        return 0

    lax.fori_loop(0, 8, last, 0)

    def last_surface(g, _):
        at = pl.multiple_of(g * n + R, R)
        surface(g, dot(BH[1, pl.ds(at, n), 0:256], wv0[:, 128:256]), STEPS - 1)
        return 0

    lax.fori_loop(0, 8 // GR, last_surface, 0)

    cell = found[...]
    row = (cell // 512) * 128 + cell % 128
    quarter = (cell // 128) % 4
    total = jnp.zeros((512, 256), F32)
    for i in range(4):
        pick = (row == lax.broadcasted_iota(jnp.int32, (512, 256), 1) + 256 * i).astype(F32).astype(BF)
        h = HIST[2 * i : 2 * i + 2].reshape(256, 128)
        hi = h.astype(BF)
        lo = (h - hi.astype(F32)).astype(BF)
        total = total + dot(pick, jnp.concatenate([hi, lo], 1))
    keep = lax.broadcasted_iota(jnp.int32, (512, 128), 1) % 4 == quarter
    out_ground[...] = jnp.where(keep, total[:, 0:128] + total[:, 128:256], 0.0)

    for c in range(3):
        for dst, W in ((out_now, WA), (out_prev, WB)):

            def store_field(xs, _):
                m = W[c, xs + 1, 8:136, :].T
                for xl in range(4):
                    for q in range(4):
                        dst[c, pl.ds(xs * 4 + xl + 256 * q, 8, stride=32), :] = m[(xl * 4 + q) * 8 : (xl * 4 + q) * 8 + 8]
                return 0

            lax.fori_loop(0, 8, store_field, 0)


def bridge_kernel(
    received, support, col, val_hbm, mass, disp, vel, acc,
    out_disp, out_vel,
    val, ground, state, sem,
):
    copies = []
    for node in range(16):
        c = pltpu.make_async_copy(val_hbm.at[node], val.at[:, :, :, node, :], sem.at[node])
        c.start()
        copies.append(c)
    rows = lax.broadcasted_iota(jnp.int32, (512, 128), 0)
    pick = jnp.concatenate([(rows == support[k : k + 1, :]).astype(F32).astype(BF) for k in range(2)], 1)
    flat = jnp.concatenate([received[128 * i : 128 * i + 128, :].T for i in range(4)], 1)
    hi = flat.astype(BF)
    lo = (flat - hi.astype(F32)).astype(BF)
    dot = functools.partial(jnp.dot, preferred_element_type=F32)
    ground[...] = jnp.sum((dot(hi, pick) + dot(lo, pick)).reshape(32, 4, 256), axis=1, keepdims=True)
    D, V, A = 0, 6, 12
    for d in range(6):
        state[D + d] = disp[:, d, :]
        state[V + d] = vel[:, d, :]
        state[A + d] = acc[:, d, :]
        state[18 + d] = mass[:, d, :]
    for c in copies:
        c.wait()
    sub = lax.broadcasted_iota(jnp.int32, (16, 128), 0)
    index = [col[:, j, :] for j in range(1, 4)]

    def step(t, _):
        new = [state[D + d] + state[V + d] + 0.5 * state[A + d] for d in range(6)]
        total = list(new)
        for j in range(4):
            for d in range(6):
                if j == 0:
                    v = new[d]
                else:
                    halves = []
                    for h in range(2):
                        ix = index[j - 1][8 * h : 8 * h + 8]
                        at = jnp.bitwise_and(ix, 7)
                        g0 = jnp.take_along_axis(new[d][0:8], at, axis=0)
                        g1 = jnp.take_along_axis(new[d][8:16], at, axis=0)
                        halves.append(jnp.where(ix >= 8, g1, g0))
                    v = jnp.concatenate(halves, 0)
                for e in range(6):
                    total[e] = total[e] + val[j, e, d] * v
        for d in range(6):
            force = -total[d]
            if d < 3:
                g = ground[t * 3 + d]
                force = force + jnp.where(sub == 0, g[:, 0:128], jnp.where(sub == 15, g[:, 128:256], 0.0))
            new_acc = state[18 + d] * force
            state[V + d] = state[V + d] + 0.5 * (state[A + d] + new_acc)
            state[A + d] = new_acc
            state[D + d] = new[d]
        return 0

    lax.fori_loop(0, STEPS, step, 0)
    for d in range(6):
        out_disp[:, d, :] = state[D + d]
        out_vel[:, d, :] = state[V + d]


def local(
    wave_now, wave_prev, shear_mod, bulk_mod, found_cell, support_row, block_col, block_val,
    mass_inv, bridge_disp, bridge_vel, bridge_acc,
):
    weights = band_weights()
    vm = pl.BlockSpec(memory_space=VMEM)
    now, before, outgoing = pl.pallas_call(
        wave_kernel,
        out_shape=[
            jax.ShapeDtypeStruct((3, 1024, 128), F32),
            jax.ShapeDtypeStruct((3, 1024, 128), F32),
            jax.ShapeDtypeStruct((512, 128), F32),
        ],
        in_specs=[vm] * 11,
        out_specs=[vm] * 3,
        scratch_shapes=[
            VMEM((3, 10, R, 128), F32),
            VMEM((3, 10, R, 128), F32),
            VMEM((2, 8, 128, 128), F32),
            VMEM((3, 10 * R, 512), BF),
            VMEM((8, GR, R, 128), F32),
            VMEM((8, 128), F32),
            VMEM((8, 128, 128), F32),
            VMEM((2, 2, 3, 64, 128), F32),
            VMEM((2, 2, 3, 64, 128), F32),
            pltpu.SemaphoreType.DMA((2, 8)),
            pltpu.SemaphoreType.DMA((2, 8)),
        ],
        compiler_params=pltpu.CompilerParams(
            collective_id=0, has_side_effects=True, vmem_limit_bytes=56 * 2**20
        ),
    )(
        wave_now.reshape(3, 1024, 128), wave_prev.reshape(3, 1024, 128),
        shear_mod.reshape(1024, 128), bulk_mod.reshape(1024, 128),
        found_cell.reshape(512, 1), *weights,
    )
    received = lax.all_to_all(
        outgoing.reshape(128, 4, 128), ("gx", "gy"), split_axis=0, concat_axis=0, tiled=True
    ).reshape(512, 128)
    deck_disp, deck_vel = pl.pallas_call(
        bridge_kernel,
        out_shape=[jax.ShapeDtypeStruct((16, 6, 128), F32)] * 2,
        in_specs=[vm] * 3 + [pl.BlockSpec(memory_space=pl.ANY)] + [vm] * 4,
        out_specs=[vm] * 2,
        scratch_shapes=[
            VMEM((4, 6, 6, 16, 128), F32),
            VMEM((32, 1, 256), F32),
            VMEM((24, 16, 128), F32),
            pltpu.SemaphoreType.DMA((16,)),
        ],
        compiler_params=pltpu.CompilerParams(vmem_limit_bytes=32 * 2**20),
    )(received, support_row, block_col, block_val, mass_inv, bridge_disp, bridge_vel, bridge_acc)
    return now.reshape(3, 32, 32, 128), before.reshape(3, 32, 32, 128), deck_disp, deck_vel


def solution(mesh):
    xy = ("gx", "gy")
    in_specs = (
        P(None, None, "gx", "gy"),
        P(None, None, "gx", "gy"),
        P(None, "gx", "gy"),
        P(None, "gx", "gy"),
        P("gx", "gy", None, None),
        P(None, xy),
        P(None, None, xy),
        P(None, None, None, None, xy),
        P(None, None, xy),
        P(None, None, xy),
        P(None, None, xy),
        P(None, None, xy),
    )
    out_specs = (
        P(None, None, "gx", "gy"),
        P(None, None, "gx", "gy"),
        P(None, None, xy),
        P(None, None, xy),
    )
    return jax.shard_map(local, mesh=mesh, in_specs=in_specs, out_specs=out_specs, check_vma=False)
```

```python
import functools

import jax
import jax.numpy as jnp
import ml_dtypes
import numpy as np
from jax import lax
from jax.experimental import pallas as pl
from jax.experimental.pallas import tpu as pltpu
from jax.sharding import PartitionSpec as P

MESH = pl.DeviceIdType.MESH
F32, BF = jnp.float32, jnp.bfloat16
STEPS = 10
GX, GY = 8, 16
R = 144
GR = 3
VMEM = pltpu.VMEM


def band(coefs, delta):
    k, n = np.arange(128)[:, None], np.arange(128)[None, :]
    dx = (k // 32 + 4 * delta) - n // 32
    dz = k % 32 - n % 32
    out = np.zeros((128, 128), np.float32)
    for (a, b), v in coefs.items():
        out[(dx == a) & (dz == b)] = v
    return out


def band_weights():
    c1 = {-2: 1, -1: -8, 1: 8, 2: -1}
    c2 = {-2: -1, -1: 16, 0: -30, 1: 16, 2: -1}
    dx = {(a, 0): v for a, v in c1.items()}
    dz = {(0, a): v for a, v in c1.items()}
    dxx = {(a, 0): v for a, v in c2.items()}
    dzz = {(0, a): v for a, v in c2.items()}
    dxz = {(a, b): v * w for a, v in c1.items() for b, w in c1.items()}
    lap = dict(dxx)
    for key, v in dzz.items():
        lap[key] = lap.get(key, 0) + v
    dxx12 = {key: 12 * v for key, v in dxx.items()}
    dzz12 = {key: 12 * v for key, v in dzz.items()}

    def two(m):
        return np.concatenate([m, m], 0)

    def beside(o):
        return np.where(np.arange(128)[:, None] < 64, band(o, 1), band(o, -1))

    def inner(ops):
        return np.concatenate([two(band(o, 0)) for o in ops], 1)

    def full(ops):
        return np.concatenate([inner(ops), np.concatenate([two(beside(o)) for o in ops], 1)], 0)

    def select(c):
        k, n = np.arange(128)[:, None], np.arange(128)[None, :]
        return two(((k % 32 == 0) & (n % 12 == c * 4 + k // 32) & (n < 120)).astype(np.float32))

    wu = full([lap, dxx12, dxz, dx])
    ww = full([lap, dxz])
    ww0 = inner([dzz12, dz])
    wv = full([lap, dx])
    wv0 = np.concatenate([inner([dz]), select(1)], 1)
    wsel = np.stack([select(0), select(2)])
    k, n = np.arange(128)[:, None], np.arange(128)[None, :]
    wslot = np.stack([two(((n == k // 4 * 4 + s) & (k < 120)).astype(np.float32)) for s in range(4)])
    return [jnp.asarray(a.astype(ml_dtypes.bfloat16)) for a in (wu, ww, ww0, wv, wv0, wsel, wslot)]


def d1(m2, m1, p1, p2):
    return (m2 - p2) + 8.0 * (p1 - m1)


def wave_kernel(
    now, prev, shear, bulk, found, wu, ww, ww0, wv, wv0, wsel, wslot,
    out_now, out_prev, out_ground,
    WA, WB, SB, BH, BHE, MU, HIST, PS, PR, G1, A1, B1, out_rows,
    send_sem, recv_sem, send_y, recv_y, send_x, recv_x,
):
    gx, gy = lax.axis_index("gx"), lax.axis_index("gy")

    def has(dx, dy):
        return (gx + dx >= 0) & (gx + dx < GX) & (gy + dy >= 0) & (gy + dy < GY)

    dirs = [(1, 0), (-1, 0), (0, 1), (0, -1), (1, 1), (1, -1), (-1, 1), (-1, -1)]
    WS = (WA, WB)
    lane = lax.broadcasted_iota(jnp.int32, (64, 128), 1)

    for W in WS:
        W[...] = jnp.zeros_like(W)
    PR[...] = jnp.zeros_like(PR)
    BH[...] = jnp.zeros_like(BH)
    BHE[...] = jnp.zeros_like(BHE)
    HIST[...] = jnp.zeros_like(HIST)

    barrier = pltpu.get_barrier_semaphore()
    count = (GX - 1) + (GY - 1)
    for i in range(1, GX):
        pl.semaphore_signal(barrier, inc=1, device_id={"gx": (gx + i) % GX, "gy": gy}, device_id_type=MESH)
    for i in range(1, GY):
        pl.semaphore_signal(barrier, inc=1, device_id={"gx": gx, "gy": (gy + i) % GY}, device_id_type=MESH)
    for dx, dy in dirs[4:]:
        ok = has(dx, dy)
        count = count + ok.astype(jnp.int32)

        @pl.when(ok)
        def _():
            pl.semaphore_signal(barrier, inc=1, device_id={"gx": gx + dx, "gy": gy + dy}, device_id_type=MESH)

    for c in range(3):
        for src, W in ((now, WA), (prev, WB)):

            def load_field(xs, _):
                rows = [src[c, pl.ds(xs * 4 + xl + 256 * q, 8, stride=32), :] for xl in range(4) for q in range(4)]
                W[c, xs + 1, 8:136, :] = jnp.concatenate(rows, 0).T
                return 0

            lax.fori_loop(0, 8, load_field, 0)
    for i, src in enumerate((shear, bulk)):

        def load_mod(xs, _):
            rows = [src[pl.ds(xs * 4 + xl + 256 * q, 8, stride=32), :] for xl in range(4) for q in range(4)]
            SB[i, xs] = jnp.concatenate(rows, 0).T * (1.0 / 12.0 if i == 0 else 1.0 / 144.0)
            return 0

        lax.fori_loop(0, 8, load_mod, 0)

    pl.semaphore_wait(barrier, count)

    def copy(p, d):
        dx, dy = dirs[d]
        W = WS[p]
        if dy == 0:
            side = 1 if dx > 0 else 0
            src, dst = PS.at[p, side], PR.at[p, 1 - side]
        else:
            y_src, y_dst = (134, 6) if dy > 0 else (8, 136)
            if dx == 0:
                src, dst = W.at[:, 1:9, pl.ds(y_src, 2), :], W.at[:, 1:9, pl.ds(y_dst, 2), :]
            else:
                x_src, x_dst = (8, 0) if dx > 0 else (1, 9)
                src, dst = W.at[0:2, x_src, pl.ds(y_src, 2), :], W.at[0:2, x_dst, pl.ds(y_dst, 2), :]
        return pltpu.make_async_remote_copy(
            src_ref=src, dst_ref=dst, send_sem=send_sem.at[p, d], recv_sem=recv_sem.at[p, d],
            device_id={"gx": gx + dx, "gy": gy + dy}, device_id_type=MESH,
        )

    X_DIRS, Y_DIRS = (0, 1, 4, 5, 6, 7), (2, 3)

    def start(p, which):
        for d in which:
            dx, dy = dirs[d]

            @pl.when(has(dx, dy))
            def _():
                copy(p, d).start()

    def send_edges_x(p):
        W = WS[p]
        for c in range(3):
            low, high = W[c, 8, 8:72, :], W[c, 8, 72:136, :]
            PS[p, 1, c] = jnp.where(lane < 64, pltpu.roll(low, 64, 1), high)
            low, high = W[c, 1, 8:72, :], W[c, 1, 72:136, :]
            PS[p, 0, c] = jnp.where(lane < 64, low, pltpu.roll(high, 64, 1))
        start(p, X_DIRS)

    def finish(p):
        for d, (dx, dy) in enumerate(dirs):

            @pl.when(has(-dx, -dy))
            def _():
                copy(p, d).wait_recv()

        for d, (dx, dy) in enumerate(dirs):

            @pl.when(has(dx, dy))
            def _():
                copy(p, d).wait_send()

        W = WS[p]
        for c in range(3):
            left, right = PR[p, 0, c], PR[p, 1, c]
            W[c, 0, 8:72, :] = pltpu.roll(left, 64, 1)
            W[c, 0, 72:136, :] = left
            W[c, 9, 8:72, :] = right
            W[c, 9, 72:136, :] = pltpu.roll(right, 64, 1)

    def halves(x):
        hi = x.astype(BF)
        return hi, (x - hi.astype(F32)).astype(BF)

    def put(B, c, x, own, up, down, n):
        hi, lo = halves(x)
        if own is not None:
            B[c, pl.ds(own, n), 0:128] = hi
            B[c, pl.ds(own, n), 128:256] = lo
        if up is not None:
            B[c, pl.ds(up, n), 320:384] = hi[:, 64:128]
            B[c, pl.ds(up, n), 448:512] = lo[:, 64:128]
        if down is not None:
            B[c, pl.ds(down, n), 256:320] = hi[:, 0:64]
            B[c, pl.ds(down, n), 384:448] = lo[:, 0:64]

    def split_inner(W):
        def body(i, _):
            own = pl.multiple_of(i * 128, 128)
            up = pl.multiple_of(i * 128 + 128, 128)
            down = pl.multiple_of(lax.rem(i + 7, 8) * 128, 128)
            for c in range(3):
                put(BH, c, W[c, i + 2, 8:136, :], own, up, down, 128)
            return 0

        lax.fori_loop(0, 6, body, 0)
        for c in range(3):
            put(BH, c, W[c, 8, 8:136, :], 6 * 128, None, 5 * 128, 128)
            put(BH, c, W[c, 1, 8:136, :], 7 * 128, 0, None, 128)

    def split_halo(W):
        for c in range(3):
            put(BH, c, W[c, 0, 8:136, :], None, 7 * 128, None, 128)
            put(BH, c, W[c, 9, 8:136, :], None, None, 6 * 128, 128)
            for xs in range(10):
                if c == 2 and xs in (0, 9):
                    continue
                edge = jnp.concatenate([W[c, xs, 0:8, :], W[c, xs, 136:144, :]], 0)
                at = (xs - 1) * 16
                inside = 1 <= xs <= 8
                cross = c < 2
                put(
                    BHE, c, edge,
                    at if inside else None,
                    at + 16 if xs <= 7 and cross else None,
                    at - 16 if xs >= 2 and cross else None,
                    16,
                )

    dot = functools.partial(jnp.dot, preferred_element_type=F32)

    def matmuls(at, n, store, surf):
        u = dot(BH[0, pl.ds(at, n), :], wu[...])
        w = dot(BH[2, pl.ds(at, n), :], ww[...])
        w0 = dot(BH[2, pl.ds(at, n), 0:256], ww0[...])
        v = dot(BH[1, pl.ds(at, n), :], wv[...])
        v0 = dot(BH[1, pl.ds(at, n), 0:256], wv0[...])
        store(0, u[:, 0:128])
        store(1, v[:, 0:128])
        store(2, w[:, 0:128])
        store(3, u[:, 128:256] + w[:, 128:256])
        store(4, u[:, 256:384] + w0[:, 0:128])
        store(5, u[:, 384:512] + w0[:, 128:256])
        store(6, v[:, 128:256])
        store(7, v0[:, 0:128])
        surf(v0[:, 128:256] + dot(BH[0, pl.ds(at, n), 0:256], wsel[0]) + dot(BH[2, pl.ds(at, n), 0:256], wsel[1]))

    group = lax.broadcasted_iota(jnp.int32, (128, 128), 1) // 12

    def keep_surface(t, xs, a):
        HIST[xs - 1] = jnp.where(group == t, a, HIST[xs - 1])

    def edge_matmuls():
        wdx, wdz = wu[:, 384:512], ww0[:, 128:256]
        e = dot(BHE[0], wdx) + dot(BHE[2, :, 0:256], wdz)
        f = dot(BHE[1], wdx)
        g = dot(BHE[1, :, 0:256], wdz)
        for k, a in ((5, e), (6, f), (7, g)):
            a = a.reshape(8, 16, 128)
            MU[k, :, 0:8, :] = a[:, 0:8]
            MU[k, :, 136:144, :] = a[:, 8:16]

    def update(xs, blocks, W, N):
        j = xs - 1
        D = (-2, -1, 1, 2)
        for yb in blocks:
            r = lambda d: pl.ds(8 + yb * 8 + d, 8)
            sh = SB[0, j, yb * 8 : yb * 8 + 8, :]
            bu = SB[1, j, yb * 8 : yb * 8 + 8, :]
            mix = [
                MU[3, j, r(0), :] + d1(*[MU[6, j, r(d), :] for d in D]),
                d1(*[MU[5, j, r(d), :] for d in D]),
                MU[4, j, r(0), :] + d1(*[MU[7, j, r(d), :] for d in D]),
            ]
            for c in range(3):
                y = [W[c, xs, r(d), :] for d in D]
                mid = W[c, xs, r(0), :]
                dyy = 16.0 * (y[1] + y[2]) - (y[0] + y[3]) - 30.0 * mid
                lap = MU[c, j, r(0), :] + dyy
                b = mix[c] + 12.0 * dyy if c == 1 else mix[c]
                N[c, xs, r(0), :] = (2.0 * mid - N[c, xs, r(0), :]) + (sh * lap + bu * b)

    def substep(p, t, send_after):
        W, N = WS[p], WS[1 - p]
        split_inner(W)

        def body(g, _):
            def store(k, a):
                MU[k, pl.ds(g * GR + 1, GR), 8:136, :] = a.reshape(GR, 128, 128)

            def surf(a):
                for i in range(GR):
                    keep_surface(t, g * GR + 2 + i, a[128 * i : 128 * i + 128])

            matmuls(pl.multiple_of(g * (GR * 128), 128), GR * 128, store, surf)
            for i in range(GR):
                update(g * GR + 2 + i, range(1, 15), W, N)
            return 0

        lax.fori_loop(0, 6 // GR, body, 0)
        finish(p)
        split_halo(W)

        def store(k, a):
            MU[k, 7, 8:136, :] = a[0:128]
            MU[k, 0, 8:136, :] = a[128:256]

        def surf(a):
            keep_surface(t, 8, a[0:128])
            keep_surface(t, 1, a[128:256])

        matmuls(6 * 128, 256, store, surf)
        edge_matmuls()
        update(1, range(16), W, N)
        update(8, range(16), W, N)

        def when_more(f):
            if send_after is True:
                f()
            else:
                pl.when(send_after)(f)

        when_more(lambda: send_edges_x(1 - p))

        def body_y(i, _):
            update(i + 2, (0, 15), W, N)
            return 0

        lax.fori_loop(0, 6, body_y, 0)
        when_more(lambda: start(1 - p, Y_DIRS))

    send_edges_x(0)
    start(0, Y_DIRS)

    def pair(i, _):
        substep(0, 2 * i - 1, True)
        substep(1, 2 * i, i < STEPS // 2 - 1)
        return 0

    lax.fori_loop(0, STEPS // 2, pair, 0)

    def last(i, _):
        total = jnp.zeros((128, 128), F32)
        for c in range(3):
            w = wv0[:, 128:256] if c == 1 else wsel[c // 2]
            total = total + dot(jnp.concatenate(halves(WA[c, i + 1, 8:136, :]), 1), w)
        keep_surface(STEPS - 1, i + 1, total)
        return 0

    lax.fori_loop(0, 8, last, 0)

    def store_fields(which):
        dst, W = ((out_now, WA), (out_prev, WB))[which]
        for c in range(3):

            def store_field(xs, _):
                m = W[c, xs + 1, 8:136, :].T
                for xl in range(4):
                    for q in range(4):
                        dst[c, pl.ds(xs * 4 + xl + 256 * q, 8, stride=32), :] = m[(xl * 4 + q) * 8 : (xl * 4 + q) * 8 + 8]
                return 0

            lax.fori_loop(0, 8, store_field, 0)

    cells = jnp.concatenate([found[...].astype(F32), jnp.zeros((124, 128), F32)], 0).T.astype(jnp.int32)
    rows = jnp.zeros((128, 128), F32)
    wide = lax.broadcasted_iota(jnp.int32, (128, 256), 1)
    narrow = lax.broadcasted_iota(jnp.int32, (128, 128), 1)
    for s in range(4):
        cell = cells[:, s : s + 1]
        row = (cell // 512) * 128 + cell % 128
        quarter = (cell // 128) % 4
        total = jnp.zeros((128, 256), F32)
        for i in range(4):
            pick = (row == wide + 256 * i).astype(F32).astype(BF)
            h = HIST[2 * i : 2 * i + 2].reshape(256, 128)
            total = total + dot(pick, jnp.concatenate(halves(h), 1))
        got = jnp.where(narrow % 4 == quarter, total[:, 0:128] + total[:, 128:256], 0.0)
        rows = rows + dot(jnp.concatenate(halves(got), 1), wslot[s])
    for i in range(GX):
        G1[:, i, :] = rows[GY * i : GY * i + GY]

    def over_y(i):
        to = (gy + i) % GY
        return pltpu.make_async_remote_copy(
            src_ref=G1.at[to], dst_ref=A1.at[gy], send_sem=send_y.at[i], recv_sem=recv_y.at[i],
            device_id={"gx": gx, "gy": to}, device_id_type=MESH,
        )

    def over_x(i):
        to = (gx + i) % GX
        return pltpu.make_async_remote_copy(
            src_ref=B1.at[to], dst_ref=out_rows.at[gx], send_sem=send_x.at[i], recv_sem=recv_x.at[i],
            device_id={"gx": to, "gy": gy}, device_id_type=MESH,
        )

    for i in range(1, GY):
        over_y(i).start()
    A1[gy] = G1[gy]
    store_fields(0)
    for i in range(1, GY):
        over_y(i).wait()
    for i in range(GX):
        B1[i] = A1[:, i, :]
    for i in range(1, GX):
        over_x(i).start()
    out_rows[gx] = B1[gx]
    store_fields(1)
    for i in range(1, GX):
        over_x(i).wait()
    out_ground[...] = out_rows[...]


def bridge_kernel(
    received, support, col, val_hbm, mass, disp, vel, acc, now, before,
    out_disp, out_vel, out_now, out_before,
    val, ground, state, sem, pass_sem,
):
    copies = []
    for node in range(16):
        c = pltpu.make_async_copy(val_hbm.at[node], val.at[:, :, :, node, :], sem.at[node])
        c.start()
        copies.append(c)
    passed = []
    for i, (src, dst) in enumerate(((now, out_now), (before, out_before))):
        c = pltpu.make_async_copy(src, dst, pass_sem.at[i])
        c.start()
        passed.append(c)
    rows = jnp.concatenate([support[0:1, :], support[1:2, :]], 1)
    pick = (lax.broadcasted_iota(jnp.int32, (128, 256), 0) == rows // 4).astype(F32).astype(BF)
    flat = received[...].T
    hi = flat.astype(BF)
    lo = (flat - hi.astype(F32)).astype(BF)
    dot = functools.partial(jnp.dot, preferred_element_type=F32)
    found = dot(hi, pick) + dot(lo, pick)
    slot = lax.broadcasted_iota(jnp.int32, (128, 256), 0) % 4 == rows % 4
    ground[...] = jnp.sum(jnp.where(slot, found, 0.0).reshape(32, 4, 256), axis=1, keepdims=True)
    D, V, A = 0, 6, 12
    for d in range(6):
        state[D + d] = disp[d]
        state[V + d] = vel[d]
        state[A + d] = acc[d]
        state[18 + d] = mass[d]
    for c in copies:
        c.wait()
    sub = lax.broadcasted_iota(jnp.int32, (16, 128), 0)
    index = [col[:, j, :] for j in range(1, 4)]

    def step(t, _):
        new = [state[D + d] + state[V + d] + 0.5 * state[A + d] for d in range(6)]
        total = list(new)
        for j in range(4):
            for d in range(6):
                if j == 0:
                    v = new[d]
                else:
                    halves = []
                    for h in range(2):
                        ix = index[j - 1][8 * h : 8 * h + 8]
                        at = jnp.bitwise_and(ix, 7)
                        g0 = jnp.take_along_axis(new[d][0:8], at, axis=0)
                        g1 = jnp.take_along_axis(new[d][8:16], at, axis=0)
                        halves.append(jnp.where(ix >= 8, g1, g0))
                    v = jnp.concatenate(halves, 0)
                for e in range(6):
                    total[e] = total[e] + val[e, d, j] * v
        for d in range(6):
            force = -total[d]
            if d < 3:
                g = ground[t * 3 + d]
                force = force + jnp.where(sub == 0, g[:, 0:128], jnp.where(sub == 15, g[:, 128:256], 0.0))
            new_acc = state[18 + d] * force
            state[V + d] = state[V + d] + 0.5 * (state[A + d] + new_acc)
            state[A + d] = new_acc
            state[D + d] = new[d]
        return 0

    lax.fori_loop(0, STEPS, step, 0)
    for d in range(6):
        out_disp[d] = state[D + d]
        out_vel[d] = state[V + d]
    for c in passed:
        c.wait()


def local(
    wave_now, wave_prev, shear_mod, bulk_mod, found_cell, support_row, block_col, block_val,
    mass_inv, bridge_disp, bridge_vel, bridge_acc,
):
    weights = band_weights()
    vm = pl.BlockSpec(memory_space=VMEM)
    now, before, outgoing = pl.pallas_call(
        wave_kernel,
        out_shape=[
            jax.ShapeDtypeStruct((3, 1024, 128), F32),
            jax.ShapeDtypeStruct((3, 1024, 128), F32),
            jax.ShapeDtypeStruct((GX, GY, 128), F32),
        ],
        in_specs=[vm] * 12,
        out_specs=[vm] * 3,
        scratch_shapes=[
            VMEM((3, 10, R, 128), F32),
            VMEM((3, 10, R, 128), F32),
            VMEM((2, 8, 128, 128), F32),
            VMEM((3, 1024, 512), BF),
            VMEM((3, 128, 512), BF),
            VMEM((8, 8, R, 128), F32),
            VMEM((8, 128, 128), F32),
            VMEM((2, 2, 3, 64, 128), F32),
            VMEM((2, 2, 3, 64, 128), F32),
            VMEM((GY, GX, 128), F32),
            VMEM((GY, GX, 128), F32),
            VMEM((GX, GY, 128), F32),
            VMEM((GX, GY, 128), F32),
            pltpu.SemaphoreType.DMA((2, 8)),
            pltpu.SemaphoreType.DMA((2, 8)),
            pltpu.SemaphoreType.DMA((GY,)),
            pltpu.SemaphoreType.DMA((GY,)),
            pltpu.SemaphoreType.DMA((GX,)),
            pltpu.SemaphoreType.DMA((GX,)),
        ],
        compiler_params=pltpu.CompilerParams(
            collective_id=0, has_side_effects=True, vmem_limit_bytes=56 * 2**20
        ),
    )(
        wave_now.reshape(3, 1024, 128), wave_prev.reshape(3, 1024, 128),
        shear_mod.reshape(1024, 128), bulk_mod.reshape(1024, 128),
        found_cell.reshape(128, 4).T, *weights,
    )
    by_dof = lambda a: jnp.transpose(a, (1, 0, 2))
    hbm = pl.BlockSpec(memory_space=pl.ANY)
    field = jax.ShapeDtypeStruct((3, 1024, 128), F32)
    deck_disp, deck_vel, now, before = pl.pallas_call(
        bridge_kernel,
        out_shape=[jax.ShapeDtypeStruct((6, 16, 128), F32)] * 2 + [field] * 2,
        in_specs=[vm] * 3 + [hbm] + [vm] * 4 + [hbm] * 2,
        out_specs=[vm] * 2 + [hbm] * 2,
        scratch_shapes=[
            VMEM((6, 6, 4, 16, 128), F32),
            VMEM((32, 1, 256), F32),
            VMEM((24, 16, 128), F32),
            pltpu.SemaphoreType.DMA((16,)),
            pltpu.SemaphoreType.DMA((2,)),
        ],
        compiler_params=pltpu.CompilerParams(vmem_limit_bytes=32 * 2**20),
    )(
        outgoing.reshape(128, 128), support_row, block_col, jnp.transpose(block_val, (0, 2, 3, 1, 4)),
        by_dof(mass_inv), by_dof(bridge_disp), by_dof(bridge_vel), by_dof(bridge_acc), now, before,
    )
    return now.reshape(3, 32, 32, 128), before.reshape(3, 32, 32, 128), by_dof(deck_disp), by_dof(deck_vel)


def solution(mesh):
    xy = ("gx", "gy")
    in_specs = (
        P(None, None, "gx", "gy"),
        P(None, None, "gx", "gy"),
        P(None, "gx", "gy"),
        P(None, "gx", "gy"),
        P("gx", "gy", None, None),
        P(None, xy),
        P(None, None, xy),
        P(None, None, None, None, xy),
        P(None, None, xy),
        P(None, None, xy),
        P(None, None, xy),
        P(None, None, xy),
    )
    out_specs = (
        P(None, None, "gx", "gy"),
        P(None, None, "gx", "gy"),
        P(None, None, xy),
        P(None, None, xy),
    )
    return jax.shard_map(local, mesh=mesh, in_specs=in_specs, out_specs=out_specs, check_vma=False)
```

```python
import functools

import jax
import jax.numpy as jnp
import ml_dtypes
import numpy as np
from jax import lax
from jax.experimental import pallas as pl
from jax.experimental.pallas import tpu as pltpu
from jax.sharding import PartitionSpec as P

MESH = pl.DeviceIdType.MESH
F32, BF = jnp.float32, jnp.bfloat16
STEPS = 10
GX, GY = 8, 16
R = 144
GR = 3
VMEM = pltpu.VMEM


def band(coefs, delta):
    k, n = np.arange(128)[:, None], np.arange(128)[None, :]
    dx = (k // 32 + 4 * delta) - n // 32
    dz = k % 32 - n % 32
    out = np.zeros((128, 128), np.float32)
    for (a, b), v in coefs.items():
        out[(dx == a) & (dz == b)] = v
    return out


def band_weights():
    c1 = {-2: 1, -1: -8, 1: 8, 2: -1}
    c2 = {-2: -1, -1: 16, 0: -30, 1: 16, 2: -1}
    dx = {(a, 0): v for a, v in c1.items()}
    dz = {(0, a): v for a, v in c1.items()}
    dxx = {(a, 0): v for a, v in c2.items()}
    dzz = {(0, a): v for a, v in c2.items()}
    dxz = {(a, b): v * w for a, v in c1.items() for b, w in c1.items()}
    lap = dict(dxx)
    for key, v in dzz.items():
        lap[key] = lap.get(key, 0) + v
    dxx12 = {key: 12 * v for key, v in dxx.items()}
    dzz12 = {key: 12 * v for key, v in dzz.items()}

    def two(m):
        return np.concatenate([m, m], 0)

    def beside(o):
        return np.where(np.arange(128)[:, None] < 64, band(o, 1), band(o, -1))

    def inner(ops):
        return np.concatenate([two(band(o, 0)) for o in ops], 1)

    def full(ops):
        return np.concatenate([inner(ops), np.concatenate([two(beside(o)) for o in ops], 1)], 0)

    def select(c):
        k, n = np.arange(128)[:, None], np.arange(128)[None, :]
        return two(((k % 32 == 0) & (n % 12 == c * 4 + k // 32) & (n < 120)).astype(np.float32))

    wu = full([lap, dxx12, dxz, dx])
    ww = full([lap, dxz])
    ww0 = inner([dzz12, dz])
    wv = full([lap, dx])
    wv0 = np.concatenate([inner([dz]), select(1)], 1)
    wsel = np.stack([select(0), select(2)])
    k, n = np.arange(128)[:, None], np.arange(128)[None, :]
    wslot = np.stack([two(((n == k // 4 * 4 + s) & (k < 120)).astype(np.float32)) for s in range(4)])
    return [jnp.asarray(a.astype(ml_dtypes.bfloat16)) for a in (wu, ww, ww0, wv, wv0, wsel, wslot)]


def d1(m2, m1, p1, p2):
    return (m2 - p2) + 8.0 * (p1 - m1)


def wave_kernel(
    now, prev, shear, bulk, found, wu, ww, ww0, wv, wv0, wsel, wslot,
    out_now, out_prev, out_ground,
    WA, WB, SB, BH, BHE, MU, HIST, PS, PR, G1, A1, B1, out_rows,
    send_sem, recv_sem, send_y, recv_y, send_x, recv_x,
):
    gx, gy = lax.axis_index("gx"), lax.axis_index("gy")

    def has(dx, dy):
        return (gx + dx >= 0) & (gx + dx < GX) & (gy + dy >= 0) & (gy + dy < GY)

    dirs = [(1, 0), (-1, 0), (0, 1), (0, -1), (1, 1), (1, -1), (-1, 1), (-1, -1)]
    WS = (WA, WB)
    lane = lax.broadcasted_iota(jnp.int32, (64, 128), 1)

    for W in WS:
        for xs in (0, 9):
            W[:, xs] = jnp.zeros((3, R, 128), F32)
        for y in (0, 136):
            W[:, 1:9, y : y + 8, :] = jnp.zeros((3, 8, 8, 128), F32)
    PR[...] = jnp.zeros_like(PR)
    HIST[...] = jnp.zeros_like(HIST)

    barrier = pltpu.get_barrier_semaphore()
    count = (GX - 1) + (GY - 1)
    for i in range(1, GX):
        pl.semaphore_signal(barrier, inc=1, device_id={"gx": (gx + i) % GX, "gy": gy}, device_id_type=MESH)
    for i in range(1, GY):
        pl.semaphore_signal(barrier, inc=1, device_id={"gx": gx, "gy": (gy + i) % GY}, device_id_type=MESH)
    for dx, dy in dirs[4:]:
        ok = has(dx, dy)
        count = count + ok.astype(jnp.int32)

        @pl.when(ok)
        def _():
            pl.semaphore_signal(barrier, inc=1, device_id={"gx": gx + dx, "gy": gy + dy}, device_id_type=MESH)

    for c in range(3):
        for src, W in ((now, WA), (prev, WB)):

            def load_field(xs, _):
                rows = [src[c, pl.ds(xs * 4 + xl + 256 * q, 8, stride=32), :] for xl in range(4) for q in range(4)]
                W[c, xs + 1, 8:136, :] = jnp.concatenate(rows, 0).T
                return 0

            lax.fori_loop(0, 8, load_field, 0)
    for i, src in enumerate((shear, bulk)):

        def load_mod(xs, _):
            rows = [src[pl.ds(xs * 4 + xl + 256 * q, 8, stride=32), :] for xl in range(4) for q in range(4)]
            SB[i, xs] = jnp.concatenate(rows, 0).T * (1.0 / 12.0 if i == 0 else 1.0 / 144.0)
            return 0

        lax.fori_loop(0, 8, load_mod, 0)

    pl.semaphore_wait(barrier, count)

    def copy(p, d):
        dx, dy = dirs[d]
        W = WS[p]
        if dy == 0:
            side = 1 if dx > 0 else 0
            src, dst = PS.at[p, side], PR.at[p, 1 - side]
        else:
            y_src, y_dst = (134, 6) if dy > 0 else (8, 136)
            if dx == 0:
                src, dst = W.at[:, 1:9, pl.ds(y_src, 2), :], W.at[:, 1:9, pl.ds(y_dst, 2), :]
            else:
                x_src, x_dst = (8, 0) if dx > 0 else (1, 9)
                src, dst = W.at[0:2, x_src, pl.ds(y_src, 2), :], W.at[0:2, x_dst, pl.ds(y_dst, 2), :]
        return pltpu.make_async_remote_copy(
            src_ref=src, dst_ref=dst, send_sem=send_sem.at[p, d], recv_sem=recv_sem.at[p, d],
            device_id={"gx": gx + dx, "gy": gy + dy}, device_id_type=MESH,
        )

    def each(dx, step):
        for d, (ex, ey) in enumerate(dirs):
            if ex == dx:
                pl.when(has(ex, ey) if step != "recv" else has(-ex, -ey))(functools.partial(act, d, step))

    def act(d, step):
        c = copy(act.p, d)
        if step == "start":
            c.start()
        elif step == "recv":
            c.wait_recv()
        else:
            c.wait_send()

    def start(p, dx):
        act.p = p
        each(dx, "start")

    def wait(p, dx_recv, dx_send):
        act.p = p
        each(dx_recv, "recv")
        each(dx_send, "send")

    def send_side(p, xs):
        W = WS[p]
        for c in range(3):
            low, high = W[c, xs, 8:72, :], W[c, xs, 72:136, :]
            if xs == 8:
                PS[p, 1, c] = jnp.where(lane < 64, pltpu.roll(low, 64, 1), high)
            else:
                PS[p, 0, c] = jnp.where(lane < 64, low, pltpu.roll(high, 64, 1))
        start(p, 1 if xs == 8 else -1)

    def halves(x):
        hi = x.astype(BF)
        return hi, (x - hi.astype(F32)).astype(BF)

    def put(B, c, x, own, up, down, n):
        hi, lo = halves(x)
        if own is not None:
            B[c, pl.ds(own, n), 0:128] = hi
            B[c, pl.ds(own, n), 128:256] = lo
        if up is not None:
            B[c, pl.ds(up, n), 320:384] = hi[:, 64:128]
            B[c, pl.ds(up, n), 448:512] = lo[:, 64:128]
        if down is not None:
            B[c, pl.ds(down, n), 256:320] = hi[:, 0:64]
            B[c, pl.ds(down, n), 384:448] = lo[:, 0:64]

    BASE = {8: 768, 1: 912}

    def split_own(W):
        def body(i, _):
            own = pl.multiple_of(i * 128, 128)
            up = pl.multiple_of(i * 128 + 128, 128)
            down = pl.multiple_of(jnp.where(i == 0, BASE[1], i * 128 - 128), 16)
            for c in range(3):
                put(BH, c, W[c, i + 2, 8:136, :], own, up, down, 128)
            return 0

        lax.fori_loop(0, 6, body, 0)
        for c in range(3):
            put(BH, c, W[c, 8, 8:136, :], BASE[8], None, 5 * 128, 128)
            put(BH, c, W[c, 1, 8:136, :], BASE[1], 0, None, 128)

    def edge(W, c, xs):
        return jnp.concatenate([W[c, xs, 0:8, :], W[c, xs, 136:144, :]], 0)

    def split_edges(W):
        for c in range(3):
            for xs in range(1, 9):
                at = (xs - 2) * 16
                cross = c < 2
                put(
                    BHE, c, edge(W, c, xs),
                    at if 2 <= xs <= 7 else None,
                    at + 16 if xs <= 6 and cross else None,
                    at - 16 if xs >= 3 and cross else None,
                    16,
                )

    def split_side(W, xs):
        base = BASE[xs]
        for c in range(3):
            if xs == 1:
                put(BH, c, W[c, 0, 8:136, :], None, base, None, 128)
            else:
                put(BH, c, W[c, 9, 8:136, :], None, None, base, 128)
            put(BH, c, edge(W, c, xs - 1), None, base + 128, None, 16)
            put(BH, c, edge(W, c, xs), base + 128, None, None, 16)
            put(BH, c, edge(W, c, xs + 1), None, None, base + 128, 16)

    dot = functools.partial(jnp.dot, preferred_element_type=F32)

    def matmuls(at, n, store, surf):
        u = dot(BH[0, pl.ds(at, n), :], wu[...])
        w = dot(BH[2, pl.ds(at, n), :], ww[...])
        w0 = dot(BH[2, pl.ds(at, n), 0:256], ww0[...])
        v = dot(BH[1, pl.ds(at, n), :], wv[...])
        v0 = dot(BH[1, pl.ds(at, n), 0:256], wv0[...])
        store(0, u[:, 0:128])
        store(1, v[:, 0:128])
        store(2, w[:, 0:128])
        store(3, u[:, 128:256] + w[:, 128:256])
        store(4, u[:, 256:384] + w0[:, 0:128])
        store(5, u[:, 384:512] + w0[:, 128:256])
        store(6, v[:, 128:256])
        store(7, v0[:, 0:128])
        surf(v0[:, 128:256] + dot(BH[0, pl.ds(at, n), 0:256], wsel[0]) + dot(BH[2, pl.ds(at, n), 0:256], wsel[1]))

    group = lax.broadcasted_iota(jnp.int32, (128, 128), 1) // 12

    def keep_surface(t, xs, a):
        HIST[xs - 1] = jnp.where(group == t, a, HIST[xs - 1])

    def edge_matmuls():
        wdx, wdz = wu[:, 384:512], ww0[:, 128:256]
        e = dot(BHE[0], wdx) + dot(BHE[2, :, 0:256], wdz)
        f = dot(BHE[1], wdx)
        g = dot(BHE[1, :, 0:256], wdz)
        for k, a in ((5, e), (6, f), (7, g)):
            a = a.reshape(6, 16, 128)
            MU[k, 1:7, 0:8, :] = a[:, 0:8]
            MU[k, 1:7, 136:144, :] = a[:, 8:16]

    def update(xs, blocks, W, N):
        j = xs - 1
        D = (-2, -1, 1, 2)
        for yb in blocks:
            r = lambda d: pl.ds(8 + yb * 8 + d, 8)
            sh = SB[0, j, yb * 8 : yb * 8 + 8, :]
            bu = SB[1, j, yb * 8 : yb * 8 + 8, :]
            mix = [
                MU[3, j, r(0), :] + d1(*[MU[6, j, r(d), :] for d in D]),
                d1(*[MU[5, j, r(d), :] for d in D]),
                MU[4, j, r(0), :] + d1(*[MU[7, j, r(d), :] for d in D]),
            ]
            for c in range(3):
                y = [W[c, xs, r(d), :] for d in D]
                mid = W[c, xs, r(0), :]
                dyy = 16.0 * (y[1] + y[2]) - (y[0] + y[3]) - 30.0 * mid
                lap = MU[c, j, r(0), :] + dyy
                b = mix[c] + 12.0 * dyy if c == 1 else mix[c]
                N[c, xs, r(0), :] = (2.0 * mid - N[c, xs, r(0), :]) + (sh * lap + bu * b)

    def substep(p, t, send_after):
        W, N = WS[p], WS[1 - p]
        split_own(W)

        def body(g, _):
            def store(k, a):
                MU[k, pl.ds(g * GR + 1, GR), 8:136, :] = a.reshape(GR, 128, 128)

            def surf(a):
                for i in range(GR):
                    keep_surface(t, g * GR + 2 + i, a[128 * i : 128 * i + 128])

            matmuls(pl.multiple_of(g * (GR * 128), 128), GR * 128, store, surf)
            for i in range(GR):
                update(g * GR + 2 + i, range(1, 15), W, N)
            return 0

        lax.fori_loop(0, 6 // GR, body, 0)
        wait(p, 0, 0)
        split_edges(W)
        edge_matmuls()

        def body_y(i, _):
            update(i + 2, (0, 15), W, N)
            return 0

        lax.fori_loop(0, 6, body_y, 0)

        def when_more(f):
            if send_after is True:
                f()
            else:
                pl.when(send_after)(f)

        def side(xs):
            out = 1 if xs == 8 else -1
            wait(p, -out, out)
            for c in range(3):
                if xs == 1:
                    left = PR[p, 0, c]
                    W[c, 0, 8:72, :] = pltpu.roll(left, 64, 1)
                    W[c, 0, 72:136, :] = left
                else:
                    right = PR[p, 1, c]
                    W[c, 9, 8:72, :] = right
                    W[c, 9, 72:136, :] = pltpu.roll(right, 64, 1)
            split_side(W, xs)

            def store(k, a):
                MU[k, xs - 1, 8:136, :] = a[0:128]
                if k >= 5:
                    MU[k, xs - 1, 0:8, :] = a[128:136]
                    MU[k, xs - 1, 136:144, :] = a[136:144]

            matmuls(BASE[xs], 144, store, lambda a: keep_surface(t, xs, a[0:128]))
            update(xs, range(16), W, N)
            when_more(lambda: send_side(1 - p, xs))

        def both(k, _):
            is_high = k == jnp.where(gx < GX // 2, 1, 0)

            @pl.when(is_high)
            def _():
                side(8)

            @pl.when(jnp.logical_not(is_high))
            def _():
                side(1)

            return 0

        lax.fori_loop(0, 2, both, 0)
        when_more(lambda: start(1 - p, 0))

    send_side(0, 8)
    send_side(0, 1)
    start(0, 0)

    def pair(i, _):
        substep(0, 2 * i - 1, True)
        substep(1, 2 * i, i < STEPS // 2 - 1)
        return 0

    lax.fori_loop(0, STEPS // 2, pair, 0)

    def last(i, _):
        total = jnp.zeros((128, 128), F32)
        for c in range(3):
            w = wv0[:, 128:256] if c == 1 else wsel[c // 2]
            total = total + dot(jnp.concatenate(halves(WA[c, i + 1, 8:136, :]), 1), w)
        keep_surface(STEPS - 1, i + 1, total)
        return 0

    lax.fori_loop(0, 8, last, 0)

    def store_fields(which):
        dst, W = ((out_now, WA), (out_prev, WB))[which]
        for c in range(3):

            def store_field(xs, _):
                m = W[c, xs + 1, 8:136, :].T
                for xl in range(4):
                    for q in range(4):
                        dst[c, pl.ds(xs * 4 + xl + 256 * q, 8, stride=32), :] = m[(xl * 4 + q) * 8 : (xl * 4 + q) * 8 + 8]
                return 0

            lax.fori_loop(0, 8, store_field, 0)

    cells = jnp.concatenate([found[...].astype(F32), jnp.zeros((124, 128), F32)], 0).T.astype(jnp.int32)
    rows = jnp.zeros((128, 128), F32)
    wide = lax.broadcasted_iota(jnp.int32, (128, 256), 1)
    narrow = lax.broadcasted_iota(jnp.int32, (128, 128), 1)
    for s in range(4):
        cell = cells[:, s : s + 1]
        row = (cell // 512) * 128 + cell % 128
        quarter = (cell // 128) % 4
        total = jnp.zeros((128, 256), F32)
        for i in range(4):
            pick = (row == wide + 256 * i).astype(F32).astype(BF)
            h = HIST[2 * i : 2 * i + 2].reshape(256, 128)
            total = total + dot(pick, jnp.concatenate(halves(h), 1))
        got = jnp.where(narrow % 4 == quarter, total[:, 0:128] + total[:, 128:256], 0.0)
        rows = rows + dot(jnp.concatenate(halves(got), 1), wslot[s])
    for i in range(GX):
        G1[:, i, :] = rows[GY * i : GY * i + GY]

    def over_y(i):
        to = (gy + i) % GY
        return pltpu.make_async_remote_copy(
            src_ref=G1.at[to], dst_ref=A1.at[gy], send_sem=send_y.at[i], recv_sem=recv_y.at[i],
            device_id={"gx": gx, "gy": to}, device_id_type=MESH,
        )

    def over_x(i):
        to = (gx + i) % GX
        return pltpu.make_async_remote_copy(
            src_ref=B1.at[to], dst_ref=out_rows.at[gx], send_sem=send_x.at[i], recv_sem=recv_x.at[i],
            device_id={"gx": to, "gy": gy}, device_id_type=MESH,
        )

    for i in range(1, GY):
        over_y(i).start()
    A1[gy] = G1[gy]
    store_fields(0)
    for i in range(1, GY):
        over_y(i).wait()
    for i in range(GX):
        B1[i] = A1[:, i, :]
    for i in range(1, GX):
        over_x(i).start()
    out_rows[gx] = B1[gx]
    store_fields(1)
    for i in range(1, GX):
        over_x(i).wait()
    out_ground[...] = out_rows[...]


def bridge_kernel(
    received, support, col, val_hbm, mass, disp, vel, acc, now, before,
    out_disp, out_vel, out_now, out_before,
    val, ground, state, sem, pass_sem,
):
    copies = []
    for node in range(16):
        c = pltpu.make_async_copy(val_hbm.at[node], val.at[:, :, :, node, :], sem.at[node])
        c.start()
        copies.append(c)
    passed = []
    for i, (src, dst) in enumerate(((now, out_now), (before, out_before))):
        c = pltpu.make_async_copy(src, dst, pass_sem.at[i])
        c.start()
        passed.append(c)
    rows = jnp.concatenate([support[0:1, :], support[1:2, :]], 1)
    pick = (lax.broadcasted_iota(jnp.int32, (128, 256), 0) == rows // 4).astype(F32).astype(BF)
    flat = received[...].T
    hi = flat.astype(BF)
    lo = (flat - hi.astype(F32)).astype(BF)
    dot = functools.partial(jnp.dot, preferred_element_type=F32)
    found = dot(hi, pick) + dot(lo, pick)
    slot = lax.broadcasted_iota(jnp.int32, (128, 256), 0) % 4 == rows % 4
    ground[...] = jnp.sum(jnp.where(slot, found, 0.0).reshape(32, 4, 256), axis=1, keepdims=True)
    D, V, A = 0, 6, 12
    for d in range(6):
        state[D + d] = disp[d]
        state[V + d] = vel[d]
        state[A + d] = acc[d]
        state[18 + d] = mass[d]
    for c in copies:
        c.wait()
    sub = lax.broadcasted_iota(jnp.int32, (16, 128), 0)
    index = [col[:, j, :] for j in range(1, 4)]

    def step(t, _):
        new = [state[D + d] + state[V + d] + 0.5 * state[A + d] for d in range(6)]
        total = list(new)
        for j in range(4):
            for d in range(6):
                if j == 0:
                    v = new[d]
                else:
                    halves = []
                    for h in range(2):
                        ix = index[j - 1][8 * h : 8 * h + 8]
                        at = jnp.bitwise_and(ix, 7)
                        g0 = jnp.take_along_axis(new[d][0:8], at, axis=0)
                        g1 = jnp.take_along_axis(new[d][8:16], at, axis=0)
                        halves.append(jnp.where(ix >= 8, g1, g0))
                    v = jnp.concatenate(halves, 0)
                for e in range(6):
                    total[e] = total[e] + val[e, d, j] * v
        for d in range(6):
            force = -total[d]
            if d < 3:
                g = ground[t * 3 + d]
                force = force + jnp.where(sub == 0, g[:, 0:128], jnp.where(sub == 15, g[:, 128:256], 0.0))
            new_acc = state[18 + d] * force
            state[V + d] = state[V + d] + 0.5 * (state[A + d] + new_acc)
            state[A + d] = new_acc
            state[D + d] = new[d]
        return 0

    lax.fori_loop(0, STEPS, step, 0)
    for d in range(6):
        out_disp[d] = state[D + d]
        out_vel[d] = state[V + d]
    for c in passed:
        c.wait()


def local(
    wave_now, wave_prev, shear_mod, bulk_mod, found_cell, support_row, block_col, block_val,
    mass_inv, bridge_disp, bridge_vel, bridge_acc,
):
    weights = band_weights()
    vm = pl.BlockSpec(memory_space=VMEM)
    now, before, outgoing = pl.pallas_call(
        wave_kernel,
        out_shape=[
            jax.ShapeDtypeStruct((3, 1024, 128), F32),
            jax.ShapeDtypeStruct((3, 1024, 128), F32),
            jax.ShapeDtypeStruct((GX, GY, 128), F32),
        ],
        in_specs=[vm] * 12,
        out_specs=[vm] * 3,
        scratch_shapes=[
            VMEM((3, 10, R, 128), F32),
            VMEM((3, 10, R, 128), F32),
            VMEM((2, 8, 128, 128), F32),
            VMEM((3, 1056, 512), BF),
            VMEM((3, 96, 512), BF),
            VMEM((8, 8, R, 128), F32),
            VMEM((8, 128, 128), F32),
            VMEM((2, 2, 3, 64, 128), F32),
            VMEM((2, 2, 3, 64, 128), F32),
            VMEM((GY, GX, 128), F32),
            VMEM((GY, GX, 128), F32),
            VMEM((GX, GY, 128), F32),
            VMEM((GX, GY, 128), F32),
            pltpu.SemaphoreType.DMA((2, 8)),
            pltpu.SemaphoreType.DMA((2, 8)),
            pltpu.SemaphoreType.DMA((GY,)),
            pltpu.SemaphoreType.DMA((GY,)),
            pltpu.SemaphoreType.DMA((GX,)),
            pltpu.SemaphoreType.DMA((GX,)),
        ],
        compiler_params=pltpu.CompilerParams(
            collective_id=0, has_side_effects=True, vmem_limit_bytes=56 * 2**20
        ),
    )(
        wave_now.reshape(3, 1024, 128), wave_prev.reshape(3, 1024, 128),
        shear_mod.reshape(1024, 128), bulk_mod.reshape(1024, 128),
        found_cell.reshape(128, 4).T, *weights,
    )
    by_dof = lambda a: jnp.transpose(a, (1, 0, 2))
    hbm = pl.BlockSpec(memory_space=pl.ANY)
    field = jax.ShapeDtypeStruct((3, 1024, 128), F32)
    deck_disp, deck_vel, now, before = pl.pallas_call(
        bridge_kernel,
        out_shape=[jax.ShapeDtypeStruct((6, 16, 128), F32)] * 2 + [field] * 2,
        in_specs=[vm] * 3 + [hbm] + [vm] * 4 + [hbm] * 2,
        out_specs=[vm] * 2 + [hbm] * 2,
        scratch_shapes=[
            VMEM((6, 6, 4, 16, 128), F32),
            VMEM((32, 1, 256), F32),
            VMEM((24, 16, 128), F32),
            pltpu.SemaphoreType.DMA((16,)),
            pltpu.SemaphoreType.DMA((2,)),
        ],
        compiler_params=pltpu.CompilerParams(vmem_limit_bytes=60 * 2**20),
    )(
        outgoing.reshape(128, 128), support_row, block_col, jnp.transpose(block_val, (0, 2, 3, 1, 4)),
        by_dof(mass_inv), by_dof(bridge_disp), by_dof(bridge_vel), by_dof(bridge_acc), now, before,
    )
    return now.reshape(3, 32, 32, 128), before.reshape(3, 32, 32, 128), by_dof(deck_disp), by_dof(deck_vel)


def solution(mesh):
    xy = ("gx", "gy")
    in_specs = (
        P(None, None, "gx", "gy"),
        P(None, None, "gx", "gy"),
        P(None, "gx", "gy"),
        P(None, "gx", "gy"),
        P("gx", "gy", None, None),
        P(None, xy),
        P(None, None, xy),
        P(None, None, None, None, xy),
        P(None, None, xy),
        P(None, None, xy),
        P(None, None, xy),
        P(None, None, xy),
    )
    out_specs = (
        P(None, None, "gx", "gy"),
        P(None, None, "gx", "gy"),
        P(None, None, xy),
        P(None, None, xy),
    )
    return jax.shard_map(local, mesh=mesh, in_specs=in_specs, out_specs=out_specs, check_vma=False)
```

```python
import functools

import jax
import jax.numpy as jnp
import ml_dtypes
import numpy as np
from jax import lax
from jax.experimental import pallas as pl
from jax.experimental.pallas import tpu as pltpu
from jax.sharding import PartitionSpec as P

MESH = pl.DeviceIdType.MESH
F32, BF = jnp.float32, jnp.bfloat16
STEPS = 10
GX, GY = 8, 16
R = 144
GR = 3
VMEM = pltpu.VMEM


def band(coefs, delta):
    k, n = np.arange(128)[:, None], np.arange(128)[None, :]
    dx = (k // 32 + 4 * delta) - n // 32
    dz = k % 32 - n % 32
    out = np.zeros((128, 128), np.float32)
    for (a, b), v in coefs.items():
        out[(dx == a) & (dz == b)] = v
    return out


def band_weights():
    c1 = {-2: 1, -1: -8, 1: 8, 2: -1}
    c2 = {-2: -1, -1: 16, 0: -30, 1: 16, 2: -1}
    dx = {(a, 0): v for a, v in c1.items()}
    dz = {(0, a): v for a, v in c1.items()}
    dxx = {(a, 0): v for a, v in c2.items()}
    dzz = {(0, a): v for a, v in c2.items()}
    dxz = {(a, b): v * w for a, v in c1.items() for b, w in c1.items()}
    lap = dict(dxx)
    for key, v in dzz.items():
        lap[key] = lap.get(key, 0) + v
    dxx12 = {key: 12 * v for key, v in dxx.items()}
    dzz12 = {key: 12 * v for key, v in dzz.items()}

    def two(m):
        return np.concatenate([m, m], 0)

    def beside(o):
        return np.where(np.arange(128)[:, None] < 64, band(o, 1), band(o, -1))

    def inner(ops):
        return np.concatenate([two(band(o, 0)) for o in ops], 1)

    def full(ops):
        return np.concatenate([inner(ops), np.concatenate([two(beside(o)) for o in ops], 1)], 0)

    def select(c):
        k, n = np.arange(128)[:, None], np.arange(128)[None, :]
        return two(((k % 32 == 0) & (n % 12 == c * 4 + k // 32) & (n < 120)).astype(np.float32))

    wu = full([lap, dxx12, dxz, dx])
    ww = full([lap, dxz])
    ww0 = inner([dzz12, dz])
    wv = full([lap, dx])
    wv0 = np.concatenate([inner([dz]), select(1)], 1)
    wsel = np.stack([select(0), select(2)])
    k, n = np.arange(128)[:, None], np.arange(128)[None, :]
    wslot = np.stack([two(((n == k // 4 * 4 + s) & (k < 120)).astype(np.float32)) for s in range(4)])
    return [jnp.asarray(a.astype(ml_dtypes.bfloat16)) for a in (wu, ww, ww0, wv, wv0, wsel, wslot)]


def d1(m2, m1, p1, p2):
    return (m2 - p2) + 8.0 * (p1 - m1)


def wave_kernel(
    now_hbm, prev_hbm, shear_hbm, bulk_hbm, found, wu_hbm, ww_hbm, ww0_hbm, wv_hbm, wv0_hbm, wsel_hbm, wslot_hbm,
    out_now, out_prev, out_ground,
    now, prev, shear, bulk, wu, ww, ww0, wv, wv0, wsel, wslot, in_sem, out_sem,
    WA, WB, SB, BH, BHE, MU, HIST, PS, PR, G1, A1, B1, out_rows,
    send_sem, recv_sem, send_y, recv_y, send_x, recv_x,
):
    gx, gy = lax.axis_index("gx"), lax.axis_index("gy")

    def has(dx, dy):
        return (gx + dx >= 0) & (gx + dx < GX) & (gy + dy >= 0) & (gy + dy < GY)

    dirs = [(1, 0), (-1, 0), (0, 1), (0, -1), (1, 1), (1, -1), (-1, 1), (-1, -1)]
    WS = (WA, WB)
    lane = lax.broadcasted_iota(jnp.int32, (64, 128), 1)

    loads = [pltpu.make_async_copy(now_hbm.at[c], now.at[c], in_sem.at[c]) for c in range(3)]
    loads += [pltpu.make_async_copy(prev_hbm.at[c], prev.at[c], in_sem.at[3 + c]) for c in range(3)]
    rest = (
        (shear_hbm, shear), (bulk_hbm, bulk), (wu_hbm, wu), (ww_hbm, ww), (ww0_hbm, ww0),
        (wv_hbm, wv), (wv0_hbm, wv0), (wsel_hbm, wsel), (wslot_hbm, wslot),
    )
    loads += [pltpu.make_async_copy(src, dst, in_sem.at[6 + i]) for i, (src, dst) in enumerate(rest)]
    for load in loads:
        load.start()

    for W in WS:
        for xs in (0, 9):
            W[:, xs] = jnp.zeros((3, R, 128), F32)
        for y in (0, 136):
            W[:, 1:9, y : y + 8, :] = jnp.zeros((3, 8, 8, 128), F32)
    PR[...] = jnp.zeros_like(PR)
    HIST[...] = jnp.zeros_like(HIST)

    barrier = pltpu.get_barrier_semaphore()
    count = (GX - 1) + (GY - 1)
    for i in range(1, GX):
        pl.semaphore_signal(barrier, inc=1, device_id={"gx": (gx + i) % GX, "gy": gy}, device_id_type=MESH)
    for i in range(1, GY):
        pl.semaphore_signal(barrier, inc=1, device_id={"gx": gx, "gy": (gy + i) % GY}, device_id_type=MESH)
    for dx, dy in dirs[4:]:
        ok = has(dx, dy)
        count = count + ok.astype(jnp.int32)

        @pl.when(ok)
        def _():
            pl.semaphore_signal(barrier, inc=1, device_id={"gx": gx + dx, "gy": gy + dy}, device_id_type=MESH)

    def turned(read, xs):
        return jnp.concatenate([read(xs * 4 + xl + 256 * q) for xl in range(4) for q in range(4)], 0).T

    def load_field(src, W, c):
        def body(i, _):
            for k in range(4):
                xs = 4 * i + k
                W[c, xs + 1, 8:136, :] = turned(lambda at: src[c, pl.ds(at, 8, stride=32), :], xs)
            return 0

        lax.fori_loop(0, 2, body, 0)

    for c in range(3):
        loads[c].wait()
        load_field(now, WA, c)
    pl.semaphore_wait(barrier, count)

    def copy(p, d):
        dx, dy = dirs[d]
        W = WS[p]
        if dy == 0:
            side = 1 if dx > 0 else 0
            src, dst = PS.at[p, side], PR.at[p, 1 - side]
        else:
            y_src, y_dst = (134, 6) if dy > 0 else (8, 136)
            if dx == 0:
                src, dst = W.at[:, 1:9, pl.ds(y_src, 2), :], W.at[:, 1:9, pl.ds(y_dst, 2), :]
            else:
                x_src, x_dst = (8, 0) if dx > 0 else (1, 9)
                src, dst = W.at[0:2, x_src, pl.ds(y_src, 2), :], W.at[0:2, x_dst, pl.ds(y_dst, 2), :]
        return pltpu.make_async_remote_copy(
            src_ref=src, dst_ref=dst, send_sem=send_sem.at[p, d], recv_sem=recv_sem.at[p, d],
            device_id={"gx": gx + dx, "gy": gy + dy}, device_id_type=MESH,
        )

    def each(dx, step):
        for d, (ex, ey) in enumerate(dirs):
            if ex == dx:
                pl.when(has(ex, ey) if step != "recv" else has(-ex, -ey))(functools.partial(act, d, step))

    def act(d, step):
        c = copy(act.p, d)
        if step == "start":
            c.start()
        elif step == "recv":
            c.wait_recv()
        else:
            c.wait_send()

    def start(p, dx):
        act.p = p
        each(dx, "start")

    def wait(p, dx_recv, dx_send):
        act.p = p
        each(dx_recv, "recv")
        each(dx_send, "send")

    def send_side(p, xs):
        W = WS[p]
        for c in range(3):
            low, high = W[c, xs, 8:72, :], W[c, xs, 72:136, :]
            if xs == 8:
                PS[p, 1, c] = jnp.where(lane < 64, pltpu.roll(low, 64, 1), high)
            else:
                PS[p, 0, c] = jnp.where(lane < 64, low, pltpu.roll(high, 64, 1))
        start(p, 1 if xs == 8 else -1)

    def halves(x):
        hi = x.astype(BF)
        return hi, (x - hi.astype(F32)).astype(BF)

    def put(B, c, x, own, up, down, n):
        hi, lo = halves(x)
        if own is not None:
            B[c, pl.ds(own, n), 0:128] = hi
            B[c, pl.ds(own, n), 128:256] = lo
        if up is not None:
            B[c, pl.ds(up, n), 320:384] = hi[:, 64:128]
            B[c, pl.ds(up, n), 448:512] = lo[:, 64:128]
        if down is not None:
            B[c, pl.ds(down, n), 256:320] = hi[:, 0:64]
            B[c, pl.ds(down, n), 384:448] = lo[:, 0:64]

    BASE = {8: 768, 1: 912}

    def split_own(W):
        def body(i, _):
            own = pl.multiple_of(i * 128, 128)
            up = pl.multiple_of(i * 128 + 128, 128)
            down = pl.multiple_of(jnp.where(i == 0, BASE[1], i * 128 - 128), 16)
            for c in range(3):
                put(BH, c, W[c, i + 2, 8:136, :], own, up, down, 128)
            return 0

        lax.fori_loop(0, 6, body, 0)
        for c in range(3):
            put(BH, c, W[c, 8, 8:136, :], BASE[8], None, 5 * 128, 128)
            put(BH, c, W[c, 1, 8:136, :], BASE[1], 0, None, 128)

    def edge(W, c, xs):
        return jnp.concatenate([W[c, xs, 0:8, :], W[c, xs, 136:144, :]], 0)

    def split_edges(W):
        for c in range(3):
            for xs in range(1, 9):
                at = (xs - 2) * 16
                cross = c < 2
                put(
                    BHE, c, edge(W, c, xs),
                    at if 2 <= xs <= 7 else None,
                    at + 16 if xs <= 6 and cross else None,
                    at - 16 if xs >= 3 and cross else None,
                    16,
                )

    def split_side(W, xs):
        base = BASE[xs]
        for c in range(3):
            if xs == 1:
                put(BH, c, W[c, 0, 8:136, :], None, base, None, 128)
            else:
                put(BH, c, W[c, 9, 8:136, :], None, None, base, 128)
            put(BH, c, edge(W, c, xs - 1), None, base + 128, None, 16)
            put(BH, c, edge(W, c, xs), base + 128, None, None, 16)
            put(BH, c, edge(W, c, xs + 1), None, None, base + 128, 16)

    dot = functools.partial(jnp.dot, preferred_element_type=F32)

    def matmuls(at, n, store, surf):
        u = dot(BH[0, pl.ds(at, n), :], wu[...])
        w = dot(BH[2, pl.ds(at, n), :], ww[...])
        w0 = dot(BH[2, pl.ds(at, n), 0:256], ww0[...])
        v = dot(BH[1, pl.ds(at, n), :], wv[...])
        v0 = dot(BH[1, pl.ds(at, n), 0:256], wv0[...])
        store(0, u[:, 0:128])
        store(1, v[:, 0:128])
        store(2, w[:, 0:128])
        store(3, u[:, 128:256] + w[:, 128:256])
        store(4, u[:, 256:384] + w0[:, 0:128])
        store(5, u[:, 384:512] + w0[:, 128:256])
        store(6, v[:, 128:256])
        store(7, v0[:, 0:128])
        surf(v0[:, 128:256] + dot(BH[0, pl.ds(at, n), 0:256], wsel[0]) + dot(BH[2, pl.ds(at, n), 0:256], wsel[1]))

    group = lax.broadcasted_iota(jnp.int32, (128, 128), 1) // 12

    def keep_surface(t, xs, a):
        HIST[xs - 1] = jnp.where(group == t, a, HIST[xs - 1])

    def edge_matmuls():
        wdx, wdz = wu[:, 384:512], ww0[:, 128:256]
        e = dot(BHE[0], wdx) + dot(BHE[2, :, 0:256], wdz)
        f = dot(BHE[1], wdx)
        g = dot(BHE[1, :, 0:256], wdz)
        for k, a in ((5, e), (6, f), (7, g)):
            a = a.reshape(6, 16, 128)
            MU[k, 1:7, 0:8, :] = a[:, 0:8]
            MU[k, 1:7, 136:144, :] = a[:, 8:16]

    def update(xs, blocks, W, N):
        j = xs - 1
        D = (-2, -1, 1, 2)
        for yb in blocks:
            r = lambda d: pl.ds(8 + yb * 8 + d, 8)
            sh = SB[0, j, yb * 8 : yb * 8 + 8, :]
            bu = SB[1, j, yb * 8 : yb * 8 + 8, :]
            mix = [
                MU[3, j, r(0), :] + d1(*[MU[6, j, r(d), :] for d in D]),
                d1(*[MU[5, j, r(d), :] for d in D]),
                MU[4, j, r(0), :] + d1(*[MU[7, j, r(d), :] for d in D]),
            ]
            for c in range(3):
                y = [W[c, xs, r(d), :] for d in D]
                mid = W[c, xs, r(0), :]
                dyy = 16.0 * (y[1] + y[2]) - (y[0] + y[3]) - 30.0 * mid
                lap = MU[c, j, r(0), :] + dyy
                b = mix[c] + 12.0 * dyy if c == 1 else mix[c]
                N[c, xs, r(0), :] = (2.0 * mid - N[c, xs, r(0), :]) + (sh * lap + bu * b)

    def substep(p, t, send_after):
        W, N = WS[p], WS[1 - p]
        split_own(W)

        def body(g, _):
            def store(k, a):
                MU[k, pl.ds(g * GR + 1, GR), 8:136, :] = a.reshape(GR, 128, 128)

            def surf(a):
                for i in range(GR):
                    keep_surface(t, g * GR + 2 + i, a[128 * i : 128 * i + 128])

            matmuls(pl.multiple_of(g * (GR * 128), 128), GR * 128, store, surf)
            for i in range(GR):
                update(g * GR + 2 + i, range(1, 15), W, N)
            return 0

        lax.fori_loop(0, 6 // GR, body, 0)
        wait(p, 0, 0)
        split_edges(W)
        edge_matmuls()

        def body_y(i, _):
            update(i + 2, (0, 15), W, N)
            return 0

        lax.fori_loop(0, 6, body_y, 0)

        def when_more(f):
            if send_after is True:
                f()
            else:
                pl.when(send_after)(f)

        def side(xs):
            out = 1 if xs == 8 else -1
            wait(p, -out, out)
            for c in range(3):
                if xs == 1:
                    left = PR[p, 0, c]
                    W[c, 0, 8:72, :] = pltpu.roll(left, 64, 1)
                    W[c, 0, 72:136, :] = left
                else:
                    right = PR[p, 1, c]
                    W[c, 9, 8:72, :] = right
                    W[c, 9, 72:136, :] = pltpu.roll(right, 64, 1)
            split_side(W, xs)

            def store(k, a):
                MU[k, xs - 1, 8:136, :] = a[0:128]
                if k >= 5:
                    MU[k, xs - 1, 0:8, :] = a[128:136]
                    MU[k, xs - 1, 136:144, :] = a[136:144]

            matmuls(BASE[xs], 144, store, lambda a: keep_surface(t, xs, a[0:128]))
            update(xs, range(16), W, N)
            when_more(lambda: send_side(1 - p, xs))

        def both(k, _):
            is_high = k == jnp.where(gx < GX // 2, 1, 0)

            @pl.when(is_high)
            def _():
                side(8)

            @pl.when(jnp.logical_not(is_high))
            def _():
                side(1)

            return 0

        lax.fori_loop(0, 2, both, 0)
        when_more(lambda: start(1 - p, 0))

    send_side(0, 8)
    send_side(0, 1)
    start(0, 0)

    for c in range(3):
        loads[3 + c].wait()
        load_field(prev, WB, c)
    loads[6].wait()
    loads[7].wait()

    def load_mod(i, _):
        for k in range(2):
            xs = 2 * i + k
            SB[0, xs] = turned(lambda at: shear[pl.ds(at, 8, stride=32), :], xs) * (1.0 / 12.0)
            SB[1, xs] = turned(lambda at: bulk[pl.ds(at, 8, stride=32), :], xs) * (1.0 / 144.0)
        return 0

    lax.fori_loop(0, 4, load_mod, 0)
    for load in loads[8:]:
        load.wait()

    def pair(i, _):
        substep(0, 2 * i - 1, True)
        substep(1, 2 * i, i < STEPS // 2 - 1)
        return 0

    lax.fori_loop(0, STEPS // 2, pair, 0)

    def last(i, _):
        total = jnp.zeros((128, 128), F32)
        for c in range(3):
            w = wv0[:, 128:256] if c == 1 else wsel[c // 2]
            total = total + dot(jnp.concatenate(halves(WA[c, i + 1, 8:136, :]), 1), w)
        keep_surface(STEPS - 1, i + 1, total)
        return 0

    lax.fori_loop(0, 8, last, 0)

    stores = [pltpu.make_async_copy(now.at[c], out_now.at[c], out_sem.at[c]) for c in range(3)]
    stores += [pltpu.make_async_copy(prev.at[c], out_prev.at[c], out_sem.at[3 + c]) for c in range(3)]

    def store_fields(which):
        dst, W = ((now, WA), (prev, WB))[which]
        for c in range(3):

            def body(i, _):
                for k in range(4):
                    xs = 4 * i + k
                    m = W[c, xs + 1, 8:136, :].T
                    for xl in range(4):
                        for q in range(4):
                            dst[c, pl.ds(xs * 4 + xl + 256 * q, 8, stride=32), :] = m[(xl * 4 + q) * 8 : (xl * 4 + q) * 8 + 8]
                return 0

            lax.fori_loop(0, 2, body, 0)
            stores[3 * which + c].start()

    cells = jnp.concatenate([found[...].astype(F32), jnp.zeros((124, 128), F32)], 0).T.astype(jnp.int32)
    rows = jnp.zeros((128, 128), F32)
    wide = lax.broadcasted_iota(jnp.int32, (128, 256), 1)
    narrow = lax.broadcasted_iota(jnp.int32, (128, 128), 1)
    for s in range(4):
        cell = cells[:, s : s + 1]
        row = (cell // 512) * 128 + cell % 128
        quarter = (cell // 128) % 4
        total = jnp.zeros((128, 256), F32)
        for i in range(4):
            pick = (row == wide + 256 * i).astype(F32).astype(BF)
            h = HIST[2 * i : 2 * i + 2].reshape(256, 128)
            total = total + dot(pick, jnp.concatenate(halves(h), 1))
        got = jnp.where(narrow % 4 == quarter, total[:, 0:128] + total[:, 128:256], 0.0)
        rows = rows + dot(jnp.concatenate(halves(got), 1), wslot[s])
    for i in range(GX):
        G1[:, i, :] = rows[GY * i : GY * i + GY]

    def over_y(i):
        to = (gy + i) % GY
        return pltpu.make_async_remote_copy(
            src_ref=G1.at[to], dst_ref=A1.at[gy], send_sem=send_y.at[i], recv_sem=recv_y.at[i],
            device_id={"gx": gx, "gy": to}, device_id_type=MESH,
        )

    def over_x(i):
        to = (gx + i) % GX
        return pltpu.make_async_remote_copy(
            src_ref=B1.at[to], dst_ref=out_rows.at[gx], send_sem=send_x.at[i], recv_sem=recv_x.at[i],
            device_id={"gx": to, "gy": gy}, device_id_type=MESH,
        )

    for i in range(1, GY):
        over_y(i).start()
    A1[gy] = G1[gy]
    store_fields(0)
    for i in range(1, GY):
        over_y(i).wait()
    for i in range(GX):
        B1[i] = A1[:, i, :]
    for i in range(1, GX):
        over_x(i).start()
    out_rows[gx] = B1[gx]
    store_fields(1)
    for i in range(1, GX):
        over_x(i).wait()
    out_ground[...] = out_rows[...]
    for store in stores:
        store.wait()


def bridge_kernel(
    received, support, col, val_hbm, mass, disp, vel, acc, now, before,
    out_disp, out_vel, out_now, out_before,
    val, ground, state, held, sem, pass_sem,
):
    copies = []
    for node in range(16):
        c = pltpu.make_async_copy(val_hbm.at[node], val.at[:, :, :, node, :], sem.at[node])
        c.start()
        copies.append(c)
    taken = [pltpu.make_async_copy(src, held.at[i], pass_sem.at[i]) for i, src in enumerate((now, before))]
    passed = [pltpu.make_async_copy(held.at[i], dst, pass_sem.at[2 + i]) for i, dst in enumerate((out_now, out_before))]
    for c in taken:
        c.start()
    rows = jnp.concatenate([support[0:1, :], support[1:2, :]], 1)
    pick = (lax.broadcasted_iota(jnp.int32, (128, 256), 0) == rows // 4).astype(F32).astype(BF)
    flat = received[...].T
    hi = flat.astype(BF)
    lo = (flat - hi.astype(F32)).astype(BF)
    dot = functools.partial(jnp.dot, preferred_element_type=F32)
    found = dot(hi, pick) + dot(lo, pick)
    slot = lax.broadcasted_iota(jnp.int32, (128, 256), 0) % 4 == rows % 4
    ground[...] = jnp.sum(jnp.where(slot, found, 0.0).reshape(32, 4, 256), axis=1, keepdims=True)
    D, V, A = 0, 6, 12
    for d in range(6):
        state[D + d] = disp[d]
        state[V + d] = vel[d]
        state[A + d] = acc[d]
        state[18 + d] = mass[d]
    for c in copies:
        c.wait()
    for i in range(2):
        taken[i].wait()
        passed[i].start()
    sub = lax.broadcasted_iota(jnp.int32, (16, 128), 0)
    index = [col[:, j, :] for j in range(1, 4)]

    def step(t, _):
        new = [state[D + d] + state[V + d] + 0.5 * state[A + d] for d in range(6)]
        total = list(new)
        for j in range(4):
            for d in range(6):
                if j == 0:
                    v = new[d]
                else:
                    halves = []
                    for h in range(2):
                        ix = index[j - 1][8 * h : 8 * h + 8]
                        at = jnp.bitwise_and(ix, 7)
                        g0 = jnp.take_along_axis(new[d][0:8], at, axis=0)
                        g1 = jnp.take_along_axis(new[d][8:16], at, axis=0)
                        halves.append(jnp.where(ix >= 8, g1, g0))
                    v = jnp.concatenate(halves, 0)
                for e in range(6):
                    total[e] = total[e] + val[e, d, j] * v
        for d in range(6):
            force = -total[d]
            if d < 3:
                g = ground[t * 3 + d]
                force = force + jnp.where(sub == 0, g[:, 0:128], jnp.where(sub == 15, g[:, 128:256], 0.0))
            new_acc = state[18 + d] * force
            state[V + d] = state[V + d] + 0.5 * (state[A + d] + new_acc)
            state[A + d] = new_acc
            state[D + d] = new[d]
        return 0

    lax.fori_loop(0, STEPS, step, 0)
    for d in range(6):
        out_disp[d] = state[D + d]
        out_vel[d] = state[V + d]
    for c in passed:
        c.wait()


def local(
    wave_now, wave_prev, shear_mod, bulk_mod, found_cell, support_row, block_col, block_val,
    mass_inv, bridge_disp, bridge_vel, bridge_acc,
):
    weights = band_weights()
    vm = pl.BlockSpec(memory_space=VMEM)
    hbm = pl.BlockSpec(memory_space=pl.ANY)
    now, before, outgoing = pl.pallas_call(
        wave_kernel,
        out_shape=[
            jax.ShapeDtypeStruct((3, 1024, 128), F32),
            jax.ShapeDtypeStruct((3, 1024, 128), F32),
            jax.ShapeDtypeStruct((GX, GY, 128), F32),
        ],
        in_specs=[hbm] * 4 + [vm] + [hbm] * 7,
        out_specs=[hbm] * 2 + [vm],
        scratch_shapes=[
            VMEM((3, 1024, 128), F32),
            VMEM((3, 1024, 128), F32),
            VMEM((1024, 128), F32),
            VMEM((1024, 128), F32),
            *[VMEM(a.shape, BF) for a in weights],
            pltpu.SemaphoreType.DMA((15,)),
            pltpu.SemaphoreType.DMA((6,)),
            VMEM((3, 10, R, 128), F32),
            VMEM((3, 10, R, 128), F32),
            VMEM((2, 8, 128, 128), F32),
            VMEM((3, 1056, 512), BF),
            VMEM((3, 96, 512), BF),
            VMEM((8, 8, R, 128), F32),
            VMEM((8, 128, 128), F32),
            VMEM((2, 2, 3, 64, 128), F32),
            VMEM((2, 2, 3, 64, 128), F32),
            VMEM((GY, GX, 128), F32),
            VMEM((GY, GX, 128), F32),
            VMEM((GX, GY, 128), F32),
            VMEM((GX, GY, 128), F32),
            pltpu.SemaphoreType.DMA((2, 8)),
            pltpu.SemaphoreType.DMA((2, 8)),
            pltpu.SemaphoreType.DMA((GY,)),
            pltpu.SemaphoreType.DMA((GY,)),
            pltpu.SemaphoreType.DMA((GX,)),
            pltpu.SemaphoreType.DMA((GX,)),
        ],
        compiler_params=pltpu.CompilerParams(
            collective_id=0, has_side_effects=True, vmem_limit_bytes=56 * 2**20
        ),
    )(
        wave_now.reshape(3, 1024, 128), wave_prev.reshape(3, 1024, 128),
        shear_mod.reshape(1024, 128), bulk_mod.reshape(1024, 128),
        found_cell.reshape(128, 4).T, *weights,
    )
    by_dof = lambda a: jnp.transpose(a, (1, 0, 2))
    field = jax.ShapeDtypeStruct((3, 1024, 128), F32)
    deck_disp, deck_vel, now, before = pl.pallas_call(
        bridge_kernel,
        out_shape=[jax.ShapeDtypeStruct((6, 16, 128), F32)] * 2 + [field] * 2,
        in_specs=[vm] * 3 + [hbm] + [vm] * 4 + [hbm] * 2,
        out_specs=[vm] * 2 + [hbm] * 2,
        scratch_shapes=[
            VMEM((6, 6, 4, 16, 128), F32),
            VMEM((32, 1, 256), F32),
            VMEM((24, 16, 128), F32),
            VMEM((2, 3, 1024, 128), F32),
            pltpu.SemaphoreType.DMA((16,)),
            pltpu.SemaphoreType.DMA((4,)),
        ],
        compiler_params=pltpu.CompilerParams(vmem_limit_bytes=60 * 2**20),
    )(
        outgoing.reshape(128, 128), support_row, block_col, jnp.transpose(block_val, (0, 2, 3, 1, 4)),
        by_dof(mass_inv), by_dof(bridge_disp), by_dof(bridge_vel), by_dof(bridge_acc), now, before,
    )
    return now.reshape(3, 32, 32, 128), before.reshape(3, 32, 32, 128), by_dof(deck_disp), by_dof(deck_vel)


def solution(mesh):
    xy = ("gx", "gy")
    in_specs = (
        P(None, None, "gx", "gy"),
        P(None, None, "gx", "gy"),
        P(None, "gx", "gy"),
        P(None, "gx", "gy"),
        P("gx", "gy", None, None),
        P(None, xy),
        P(None, None, xy),
        P(None, None, None, None, xy),
        P(None, None, xy),
        P(None, None, xy),
        P(None, None, xy),
        P(None, None, xy),
    )
    out_specs = (
        P(None, None, "gx", "gy"),
        P(None, None, "gx", "gy"),
        P(None, None, xy),
        P(None, None, xy),
    )
    return jax.shard_map(local, mesh=mesh, in_specs=in_specs, out_specs=out_specs, check_vma=False)
```

```python
import functools

import jax
import jax.numpy as jnp
import ml_dtypes
import numpy as np
from jax import lax
from jax.experimental import pallas as pl
from jax.experimental.pallas import tpu as pltpu
from jax.sharding import PartitionSpec as P

MESH = pl.DeviceIdType.MESH
F32, BF = jnp.float32, jnp.bfloat16
STEPS = 10
GX, GY = 8, 16
R = 144
GR = 3
VMEM = pltpu.VMEM


def band(coefs, delta):
    k, n = np.arange(128)[:, None], np.arange(128)[None, :]
    dx = (k // 32 + 4 * delta) - n // 32
    dz = k % 32 - n % 32
    out = np.zeros((128, 128), np.float32)
    for (a, b), v in coefs.items():
        out[(dx == a) & (dz == b)] = v
    return out


def band_weights():
    c1 = {-2: 1, -1: -8, 1: 8, 2: -1}
    c2 = {-2: -1, -1: 16, 0: -30, 1: 16, 2: -1}
    dx = {(a, 0): v for a, v in c1.items()}
    dz = {(0, a): v for a, v in c1.items()}
    dxx = {(a, 0): v for a, v in c2.items()}
    dzz = {(0, a): v for a, v in c2.items()}
    dxz = {(a, b): v * w for a, v in c1.items() for b, w in c1.items()}
    lap = dict(dxx)
    for key, v in dzz.items():
        lap[key] = lap.get(key, 0) + v
    dxx12 = {key: 12 * v for key, v in dxx.items()}
    dzz12 = {key: 12 * v for key, v in dzz.items()}

    def two(m):
        return np.concatenate([m, m], 0)

    def beside(o):
        return np.where(np.arange(128)[:, None] < 64, band(o, 1), band(o, -1))

    def inner(ops):
        return np.concatenate([two(band(o, 0)) for o in ops], 1)

    def full(ops):
        return np.concatenate([inner(ops), np.concatenate([two(beside(o)) for o in ops], 1)], 0)

    def select(c):
        k, n = np.arange(128)[:, None], np.arange(128)[None, :]
        return two(((k % 32 == 0) & (n % 12 == c * 4 + k // 32) & (n < 120)).astype(np.float32))

    wu = full([lap, dxx12, dxz, dx])
    ww = full([lap, dxz])
    ww0 = inner([dzz12, dz])
    wv = full([lap, dx])
    wv0 = np.concatenate([inner([dz]), select(1)], 1)
    wsel = np.stack([select(0), select(2)])
    k, n = np.arange(128)[:, None], np.arange(128)[None, :]
    wslot = np.stack([two(((n == k // 4 * 4 + s) & (k < 120)).astype(np.float32)) for s in range(4)])
    return [jnp.asarray(a.astype(ml_dtypes.bfloat16)) for a in (wu, ww, ww0, wv, wv0, wsel, wslot)]


def d1(m2, m1, p1, p2):
    return (m2 - p2) + 8.0 * (p1 - m1)


def wave_kernel(
    now_hbm, prev_hbm, shear_hbm, bulk_hbm, found, wu_hbm, ww_hbm, ww0_hbm, wv_hbm, wv0_hbm, wsel_hbm, wslot_hbm,
    out_now, out_prev, out_ground,
    now, prev, shear, bulk, wu, ww, ww0, wv, wv0, wsel, wslot, in_sem, out_sem,
    WA, WB, SB, BH, BHE, MU, HIST, PS, PR, G1, A1, B1, out_rows,
    send_sem, recv_sem, send_y, recv_y, send_x, recv_x,
):
    gx, gy = lax.axis_index("gx"), lax.axis_index("gy")

    def has(dx, dy):
        return (gx + dx >= 0) & (gx + dx < GX) & (gy + dy >= 0) & (gy + dy < GY)

    dirs = [
        (1, 1, 8), (1, -1, 8), (0, 1, 8), (0, -1, 8), (1, 0, 8),
        (-1, 1, 1), (-1, -1, 1), (0, 1, 1), (0, -1, 1), (-1, 0, 1),
        (0, 1, 0), (0, -1, 0),
    ]
    WS = (WA, WB)
    lane = lax.broadcasted_iota(jnp.int32, (64, 128), 1)

    loads = [pltpu.make_async_copy(now_hbm.at[c], now.at[c], in_sem.at[c]) for c in range(3)]
    loads += [pltpu.make_async_copy(prev_hbm.at[c], prev.at[c], in_sem.at[3 + c]) for c in range(3)]
    rest = (
        (shear_hbm, shear), (bulk_hbm, bulk), (wu_hbm, wu), (ww_hbm, ww), (ww0_hbm, ww0),
        (wv_hbm, wv), (wv0_hbm, wv0), (wsel_hbm, wsel), (wslot_hbm, wslot),
    )
    loads += [pltpu.make_async_copy(src, dst, in_sem.at[6 + i]) for i, (src, dst) in enumerate(rest)]
    for load in loads:
        load.start()

    for W in WS:
        for xs in (0, 9):
            W[:, xs] = jnp.zeros((3, R, 128), F32)
        for y in (0, 136):
            W[:, 1:9, y : y + 8, :] = jnp.zeros((3, 8, 8, 128), F32)
    PR[...] = jnp.zeros_like(PR)
    HIST[...] = jnp.zeros_like(HIST)

    barrier = pltpu.get_barrier_semaphore()
    count = (GX - 1) + (GY - 1)
    for i in range(1, GX):
        pl.semaphore_signal(barrier, inc=1, device_id={"gx": (gx + i) % GX, "gy": gy}, device_id_type=MESH)
    for i in range(1, GY):
        pl.semaphore_signal(barrier, inc=1, device_id={"gx": gx, "gy": (gy + i) % GY}, device_id_type=MESH)
    for dx, dy in ((1, 1), (1, -1), (-1, 1), (-1, -1)):
        ok = has(dx, dy)
        count = count + ok.astype(jnp.int32)

        @pl.when(ok)
        def _():
            pl.semaphore_signal(barrier, inc=1, device_id={"gx": gx + dx, "gy": gy + dy}, device_id_type=MESH)

    def turned(read, xs):
        return jnp.concatenate([read(xs * 4 + xl + 256 * q) for xl in range(4) for q in range(4)], 0).T

    def load_field(src, W, c):
        def body(i, _):
            for k in range(4):
                xs = 4 * i + k
                W[c, xs + 1, 8:136, :] = turned(lambda at: src[c, pl.ds(at, 8, stride=32), :], xs)
            return 0

        lax.fori_loop(0, 2, body, 0)

    for c in range(3):
        loads[c].wait()
        load_field(now, WA, c)
    pl.semaphore_wait(barrier, count)

    def copy(p, d):
        dx, dy, slab = dirs[d]
        W = WS[p]
        if dy == 0:
            side = 1 if dx > 0 else 0
            src, dst = PS.at[p, side], PR.at[p, 1 - side]
        else:
            y_src, y_dst = (134, 6) if dy > 0 else (8, 136)
            if dx == 0:
                slabs = pl.ds(slab, 1) if slab else pl.ds(2, 6)
                src, dst = W.at[:, slabs, pl.ds(y_src, 2), :], W.at[:, slabs, pl.ds(y_dst, 2), :]
            else:
                x_src, x_dst = (8, 0) if dx > 0 else (1, 9)
                src, dst = W.at[0:2, x_src, pl.ds(y_src, 2), :], W.at[0:2, x_dst, pl.ds(y_dst, 2), :]
        return pltpu.make_async_remote_copy(
            src_ref=src, dst_ref=dst, send_sem=send_sem.at[p, d], recv_sem=recv_sem.at[p, d],
            device_id={"gx": gx + dx, "gy": gy + dy}, device_id_type=MESH,
        )

    def start(p, slab):
        for d, (dx, dy, after) in enumerate(dirs):
            if after == slab:

                @pl.when(has(dx, dy))
                def _():
                    copy(p, d).start()

    def wait(p, dx_recv, dx_send):
        for d, (dx, dy, _) in enumerate(dirs):
            if dx == dx_recv:

                @pl.when(has(-dx, -dy))
                def _():
                    copy(p, d).wait_recv()

            if dx == dx_send:

                @pl.when(has(dx, dy))
                def _():
                    copy(p, d).wait_send()

    def send_side(p, xs):
        W = WS[p]
        for c in range(3):
            low, high = W[c, xs, 8:72, :], W[c, xs, 72:136, :]
            if xs == 8:
                PS[p, 1, c] = jnp.where(lane < 64, pltpu.roll(low, 64, 1), high)
            else:
                PS[p, 0, c] = jnp.where(lane < 64, low, pltpu.roll(high, 64, 1))
        start(p, xs)

    def halves(x):
        hi = x.astype(BF)
        return hi, (x - hi.astype(F32)).astype(BF)

    def put(B, c, x, own, up, down, n):
        hi, lo = halves(x)
        if own is not None:
            B[c, pl.ds(own, n), 0:128] = hi
            B[c, pl.ds(own, n), 128:256] = lo
        if up is not None:
            B[c, pl.ds(up, n), 320:384] = hi[:, 64:128]
            B[c, pl.ds(up, n), 448:512] = lo[:, 64:128]
        if down is not None:
            B[c, pl.ds(down, n), 256:320] = hi[:, 0:64]
            B[c, pl.ds(down, n), 384:448] = lo[:, 0:64]

    BASE = {8: 768, 1: 912}

    def split_own(W):
        def body(i, _):
            own = pl.multiple_of(i * 128, 128)
            up = pl.multiple_of(i * 128 + 128, 128)
            down = pl.multiple_of(jnp.where(i == 0, BASE[1], i * 128 - 128), 16)
            for c in range(3):
                put(BH, c, W[c, i + 2, 8:136, :], own, up, down, 128)
            return 0

        lax.fori_loop(0, 6, body, 0)
        for c in range(3):
            put(BH, c, W[c, 8, 8:136, :], BASE[8], None, 5 * 128, 128)
            put(BH, c, W[c, 1, 8:136, :], BASE[1], 0, None, 128)

    def edge(W, c, xs):
        return jnp.concatenate([W[c, xs, 0:8, :], W[c, xs, 136:144, :]], 0)

    def split_edges(W):
        for c in range(3):
            for xs in range(1, 9):
                at = (xs - 2) * 16
                cross = c < 2
                put(
                    BHE, c, edge(W, c, xs),
                    at if 2 <= xs <= 7 else None,
                    at + 16 if xs <= 6 and cross else None,
                    at - 16 if xs >= 3 and cross else None,
                    16,
                )

    def split_side(W, xs):
        base = BASE[xs]
        for c in range(3):
            if xs == 1:
                put(BH, c, W[c, 0, 8:136, :], None, base, None, 128)
            else:
                put(BH, c, W[c, 9, 8:136, :], None, None, base, 128)
            put(BH, c, edge(W, c, xs - 1), None, base + 128, None, 16)
            put(BH, c, edge(W, c, xs), base + 128, None, None, 16)
            put(BH, c, edge(W, c, xs + 1), None, None, base + 128, 16)

    dot = functools.partial(jnp.dot, preferred_element_type=F32)

    def matmuls(at, n, store, surf):
        u = dot(BH[0, pl.ds(at, n), :], wu[...])
        w = dot(BH[2, pl.ds(at, n), :], ww[...])
        w0 = dot(BH[2, pl.ds(at, n), 0:256], ww0[...])
        v = dot(BH[1, pl.ds(at, n), :], wv[...])
        v0 = dot(BH[1, pl.ds(at, n), 0:256], wv0[...])
        store(0, u[:, 0:128])
        store(1, v[:, 0:128])
        store(2, w[:, 0:128])
        store(3, u[:, 128:256] + w[:, 128:256])
        store(4, u[:, 256:384] + w0[:, 0:128])
        store(5, u[:, 384:512] + w0[:, 128:256])
        store(6, v[:, 128:256])
        store(7, v0[:, 0:128])
        surf(v0[:, 128:256] + dot(BH[0, pl.ds(at, n), 0:256], wsel[0]) + dot(BH[2, pl.ds(at, n), 0:256], wsel[1]))

    group = lax.broadcasted_iota(jnp.int32, (128, 128), 1) // 12

    def keep_surface(t, xs, a):
        HIST[xs - 1] = jnp.where(group == t, a, HIST[xs - 1])

    def edge_matmuls():
        wdx, wdz = wu[:, 384:512], ww0[:, 128:256]
        e = dot(BHE[0], wdx) + dot(BHE[2, :, 0:256], wdz)
        f = dot(BHE[1], wdx)
        g = dot(BHE[1, :, 0:256], wdz)
        for k, a in ((5, e), (6, f), (7, g)):
            a = a.reshape(6, 16, 128)
            MU[k, 1:7, 0:8, :] = a[:, 0:8]
            MU[k, 1:7, 136:144, :] = a[:, 8:16]

    def update(xs, blocks, W, N):
        j = xs - 1
        D = (-2, -1, 1, 2)
        for yb in blocks:
            r = lambda d: pl.ds(8 + yb * 8 + d, 8)
            sh = SB[0, j, yb * 8 : yb * 8 + 8, :]
            bu = SB[1, j, yb * 8 : yb * 8 + 8, :]
            mix = [
                MU[3, j, r(0), :] + d1(*[MU[6, j, r(d), :] for d in D]),
                d1(*[MU[5, j, r(d), :] for d in D]),
                MU[4, j, r(0), :] + d1(*[MU[7, j, r(d), :] for d in D]),
            ]
            for c in range(3):
                y = [W[c, xs, r(d), :] for d in D]
                mid = W[c, xs, r(0), :]
                dyy = 16.0 * (y[1] + y[2]) - (y[0] + y[3]) - 30.0 * mid
                lap = MU[c, j, r(0), :] + dyy
                b = mix[c] + 12.0 * dyy if c == 1 else mix[c]
                N[c, xs, r(0), :] = (2.0 * mid - N[c, xs, r(0), :]) + (sh * lap + bu * b)

    stores = [pltpu.make_async_copy(now.at[c], out_now.at[c], out_sem.at[c]) for c in range(3)]
    stores += [pltpu.make_async_copy(prev.at[c], out_prev.at[c], out_sem.at[3 + c]) for c in range(3)]

    def store_fields(which, components):
        dst, W = ((now, WA), (prev, WB))[which]
        for c in components:

            def body(i, _):
                for k in range(4):
                    xs = 4 * i + k
                    m = W[c, xs + 1, 8:136, :].T
                    for xl in range(4):
                        for q in range(4):
                            dst[c, pl.ds(xs * 4 + xl + 256 * q, 8, stride=32), :] = m[(xl * 4 + q) * 8 : (xl * 4 + q) * 8 + 8]
                return 0

            lax.fori_loop(0, 2, body, 0)
            stores[3 * which + c].start()

    def substep(p, t, send_after):
        W, N = WS[p], WS[1 - p]
        split_own(W)

        def body(g, _):
            def store(k, a):
                MU[k, pl.ds(g * GR + 1, GR), 8:136, :] = a.reshape(GR, 128, 128)

            def surf(a):
                for i in range(GR):
                    keep_surface(t, g * GR + 2 + i, a[128 * i : 128 * i + 128])

            matmuls(pl.multiple_of(g * (GR * 128), 128), GR * 128, store, surf)
            for i in range(GR):
                update(g * GR + 2 + i, range(1, 15), W, N)
            return 0

        lax.fori_loop(0, 6 // GR, body, 0)
        wait(p, 0, 0)
        split_edges(W)
        edge_matmuls()

        def body_y(i, _):
            update(i + 2, (0, 15), W, N)
            return 0

        lax.fori_loop(0, 6, body_y, 0)

        def when_more(f):
            if send_after is True:
                f()
            else:
                pl.when(send_after)(f)

        when_more(lambda: start(1 - p, 0))

        def side(xs):
            out = 1 if xs == 8 else -1
            wait(p, -out, out)
            for c in range(3):
                if xs == 1:
                    left = PR[p, 0, c]
                    W[c, 0, 8:72, :] = pltpu.roll(left, 64, 1)
                    W[c, 0, 72:136, :] = left
                else:
                    right = PR[p, 1, c]
                    W[c, 9, 8:72, :] = right
                    W[c, 9, 72:136, :] = pltpu.roll(right, 64, 1)
            split_side(W, xs)

            def store(k, a):
                MU[k, xs - 1, 8:136, :] = a[0:128]
                if k >= 5:
                    MU[k, xs - 1, 0:8, :] = a[128:136]
                    MU[k, xs - 1, 136:144, :] = a[136:144]

            matmuls(BASE[xs], 144, store, lambda a: keep_surface(t, xs, a[0:128]))
            update(xs, range(16), W, N)
            when_more(lambda: send_side(1 - p, xs))

        def both(k, _):
            is_high = k == jnp.where(gx < GX // 2, 1, 0)

            @pl.when(is_high)
            def _():
                side(8)

            @pl.when(jnp.logical_not(is_high))
            def _():
                side(1)

            return 0

        if p == 1:

            @pl.when(jnp.logical_not(send_after))
            def _():
                store_fields(1, range(3))

        lax.fori_loop(0, 2, both, 0)

    send_side(0, 8)
    send_side(0, 1)
    start(0, 0)

    for c in range(3):
        loads[3 + c].wait()
        load_field(prev, WB, c)
    loads[6].wait()
    loads[7].wait()

    def load_mod(i, _):
        for k in range(2):
            xs = 2 * i + k
            SB[0, xs] = turned(lambda at: shear[pl.ds(at, 8, stride=32), :], xs) * (1.0 / 12.0)
            SB[1, xs] = turned(lambda at: bulk[pl.ds(at, 8, stride=32), :], xs) * (1.0 / 144.0)
        return 0

    lax.fori_loop(0, 4, load_mod, 0)
    for load in loads[8:]:
        load.wait()

    def pair(i, _):
        substep(0, 2 * i - 1, True)
        substep(1, 2 * i, i < STEPS // 2 - 1)
        return 0

    lax.fori_loop(0, STEPS // 2, pair, 0)

    def last(i, _):
        total = jnp.zeros((128, 128), F32)
        for c in range(3):
            w = wv0[:, 128:256] if c == 1 else wsel[c // 2]
            total = total + dot(jnp.concatenate(halves(WA[c, i + 1, 8:136, :]), 1), w)
        keep_surface(STEPS - 1, i + 1, total)
        return 0

    lax.fori_loop(0, 8, last, 0)

    cells = jnp.concatenate([found[...].astype(F32), jnp.zeros((124, 128), F32)], 0).T.astype(jnp.int32)
    rows = jnp.zeros((128, 128), F32)
    wide = lax.broadcasted_iota(jnp.int32, (128, 256), 1)
    narrow = lax.broadcasted_iota(jnp.int32, (128, 128), 1)
    for s in range(4):
        cell = cells[:, s : s + 1]
        row = (cell // 512) * 128 + cell % 128
        quarter = (cell // 128) % 4
        total = jnp.zeros((128, 256), F32)
        for i in range(4):
            pick = (row == wide + 256 * i).astype(F32).astype(BF)
            h = HIST[2 * i : 2 * i + 2].reshape(256, 128)
            total = total + dot(pick, jnp.concatenate(halves(h), 1))
        got = jnp.where(narrow % 4 == quarter, total[:, 0:128] + total[:, 128:256], 0.0)
        rows = rows + dot(jnp.concatenate(halves(got), 1), wslot[s])
    for i in range(GX):
        G1[:, i, :] = rows[GY * i : GY * i + GY]

    def over_y(i):
        to = (gy + i) % GY
        return pltpu.make_async_remote_copy(
            src_ref=G1.at[to], dst_ref=A1.at[gy], send_sem=send_y.at[i], recv_sem=recv_y.at[i],
            device_id={"gx": gx, "gy": to}, device_id_type=MESH,
        )

    def over_x(i):
        to = (gx + i) % GX
        return pltpu.make_async_remote_copy(
            src_ref=B1.at[to], dst_ref=out_rows.at[gx], send_sem=send_x.at[i], recv_sem=recv_x.at[i],
            device_id={"gx": to, "gy": gy}, device_id_type=MESH,
        )

    for i in range(1, GY):
        over_y(i).start()
    A1[gy] = G1[gy]
    store_fields(0, range(2))
    for i in range(1, GY):
        over_y(i).wait()
    for i in range(GX):
        B1[i] = A1[:, i, :]
    for i in range(1, GX):
        over_x(i).start()
    out_rows[gx] = B1[gx]
    store_fields(0, range(2, 3))
    for i in range(1, GX):
        over_x(i).wait()
    out_ground[...] = out_rows[...]
    for store in stores:
        store.wait()


def bridge_kernel(
    received, support, col, val_hbm, mass, disp, vel, acc, now, before,
    out_disp, out_vel, out_now, out_before,
    val, ground, state, held, sem, pass_sem,
):
    copies = []
    for node in range(16):
        c = pltpu.make_async_copy(val_hbm.at[node], val.at[:, :, :, node, :], sem.at[node])
        c.start()
        copies.append(c)
    taken = [pltpu.make_async_copy(src, held.at[i], pass_sem.at[i]) for i, src in enumerate((now, before))]
    passed = [pltpu.make_async_copy(held.at[i], dst, pass_sem.at[2 + i]) for i, dst in enumerate((out_now, out_before))]
    rows = jnp.concatenate([support[0:1, :], support[1:2, :]], 1)
    pick = (lax.broadcasted_iota(jnp.int32, (128, 256), 0) == rows // 4).astype(F32).astype(BF)
    flat = received[...].T
    hi = flat.astype(BF)
    lo = (flat - hi.astype(F32)).astype(BF)
    dot = functools.partial(jnp.dot, preferred_element_type=F32)
    found = dot(hi, pick) + dot(lo, pick)
    slot = lax.broadcasted_iota(jnp.int32, (128, 256), 0) % 4 == rows % 4
    ground[...] = jnp.sum(jnp.where(slot, found, 0.0).reshape(32, 4, 256), axis=1, keepdims=True)
    D, V, A = 0, 6, 12
    for d in range(6):
        state[D + d] = disp[d]
        state[V + d] = vel[d]
        state[A + d] = acc[d]
        state[18 + d] = mass[d]
    for c in copies:
        c.wait()
    for c in taken:
        c.start()
    sub = lax.broadcasted_iota(jnp.int32, (16, 128), 0)
    index = [col[:, j, :] for j in range(1, 4)]

    def step(t, _):
        new = [state[D + d] + state[V + d] + 0.5 * state[A + d] for d in range(6)]
        total = list(new)
        for j in range(4):
            for d in range(6):
                if j == 0:
                    v = new[d]
                else:
                    halves = []
                    for h in range(2):
                        ix = index[j - 1][8 * h : 8 * h + 8]
                        at = jnp.bitwise_and(ix, 7)
                        g0 = jnp.take_along_axis(new[d][0:8], at, axis=0)
                        g1 = jnp.take_along_axis(new[d][8:16], at, axis=0)
                        halves.append(jnp.where(ix >= 8, g1, g0))
                    v = jnp.concatenate(halves, 0)
                for e in range(6):
                    total[e] = total[e] + val[e, d, j] * v
        for d in range(6):
            force = -total[d]
            if d < 3:
                g = ground[t * 3 + d]
                force = force + jnp.where(sub == 0, g[:, 0:128], jnp.where(sub == 15, g[:, 128:256], 0.0))
            new_acc = state[18 + d] * force
            state[V + d] = state[V + d] + 0.5 * (state[A + d] + new_acc)
            state[A + d] = new_acc
            state[D + d] = new[d]
        return 0

    lax.fori_loop(0, STEPS // 2, step, 0)
    for i in range(2):
        taken[i].wait()
        passed[i].start()
    lax.fori_loop(STEPS // 2, STEPS, step, 0)
    for d in range(6):
        out_disp[d] = state[D + d]
        out_vel[d] = state[V + d]
    for c in passed:
        c.wait()


def local(
    wave_now, wave_prev, shear_mod, bulk_mod, found_cell, support_row, block_col, block_val,
    mass_inv, bridge_disp, bridge_vel, bridge_acc,
):
    weights = band_weights()
    vm = pl.BlockSpec(memory_space=VMEM)
    hbm = pl.BlockSpec(memory_space=pl.ANY)
    now, before, outgoing = pl.pallas_call(
        wave_kernel,
        out_shape=[
            jax.ShapeDtypeStruct((3, 1024, 128), F32),
            jax.ShapeDtypeStruct((3, 1024, 128), F32),
            jax.ShapeDtypeStruct((GX, GY, 128), F32),
        ],
        in_specs=[hbm] * 4 + [vm] + [hbm] * 7,
        out_specs=[hbm] * 2 + [vm],
        scratch_shapes=[
            VMEM((3, 1024, 128), F32),
            VMEM((3, 1024, 128), F32),
            VMEM((1024, 128), F32),
            VMEM((1024, 128), F32),
            *[VMEM(a.shape, BF) for a in weights],
            pltpu.SemaphoreType.DMA((15,)),
            pltpu.SemaphoreType.DMA((6,)),
            VMEM((3, 10, R, 128), F32),
            VMEM((3, 10, R, 128), F32),
            VMEM((2, 8, 128, 128), F32),
            VMEM((3, 1056, 512), BF),
            VMEM((3, 96, 512), BF),
            VMEM((8, 8, R, 128), F32),
            VMEM((8, 128, 128), F32),
            VMEM((2, 2, 3, 64, 128), F32),
            VMEM((2, 2, 3, 64, 128), F32),
            VMEM((GY, GX, 128), F32),
            VMEM((GY, GX, 128), F32),
            VMEM((GX, GY, 128), F32),
            VMEM((GX, GY, 128), F32),
            pltpu.SemaphoreType.DMA((2, 12)),
            pltpu.SemaphoreType.DMA((2, 12)),
            pltpu.SemaphoreType.DMA((GY,)),
            pltpu.SemaphoreType.DMA((GY,)),
            pltpu.SemaphoreType.DMA((GX,)),
            pltpu.SemaphoreType.DMA((GX,)),
        ],
        compiler_params=pltpu.CompilerParams(
            collective_id=0, has_side_effects=True, vmem_limit_bytes=56 * 2**20
        ),
    )(
        wave_now.reshape(3, 1024, 128), wave_prev.reshape(3, 1024, 128),
        shear_mod.reshape(1024, 128), bulk_mod.reshape(1024, 128),
        found_cell.reshape(128, 4).T, *weights,
    )
    by_dof = lambda a: jnp.transpose(a, (1, 0, 2))
    field = jax.ShapeDtypeStruct((3, 1024, 128), F32)
    deck_disp, deck_vel, now, before = pl.pallas_call(
        bridge_kernel,
        out_shape=[jax.ShapeDtypeStruct((6, 16, 128), F32)] * 2 + [field] * 2,
        in_specs=[vm] * 3 + [hbm] + [vm] * 4 + [hbm] * 2,
        out_specs=[vm] * 2 + [hbm] * 2,
        scratch_shapes=[
            VMEM((6, 6, 4, 16, 128), F32),
            VMEM((32, 1, 256), F32),
            VMEM((24, 16, 128), F32),
            VMEM((2, 3, 1024, 128), F32),
            pltpu.SemaphoreType.DMA((16,)),
            pltpu.SemaphoreType.DMA((4,)),
        ],
        compiler_params=pltpu.CompilerParams(vmem_limit_bytes=52 * 2**20),
    )(
        outgoing.reshape(128, 128), support_row, block_col, jnp.transpose(block_val, (0, 2, 3, 1, 4)),
        by_dof(mass_inv), by_dof(bridge_disp), by_dof(bridge_vel), by_dof(bridge_acc), now, before,
    )
    return now.reshape(3, 32, 32, 128), before.reshape(3, 32, 32, 128), by_dof(deck_disp), by_dof(deck_vel)


def solution(mesh):
    xy = ("gx", "gy")
    in_specs = (
        P(None, None, "gx", "gy"),
        P(None, None, "gx", "gy"),
        P(None, "gx", "gy"),
        P(None, "gx", "gy"),
        P("gx", "gy", None, None),
        P(None, xy),
        P(None, None, xy),
        P(None, None, None, None, xy),
        P(None, None, xy),
        P(None, None, xy),
        P(None, None, xy),
        P(None, None, xy),
    )
    out_specs = (
        P(None, None, "gx", "gy"),
        P(None, None, "gx", "gy"),
        P(None, None, xy),
        P(None, None, xy),
    )
    return jax.shard_map(local, mesh=mesh, in_specs=in_specs, out_specs=out_specs, check_vma=False)
```

```python
import functools

import jax
import jax.numpy as jnp
import ml_dtypes
import numpy as np
from jax import lax
from jax.experimental import pallas as pl
from jax.experimental.pallas import tpu as pltpu
from jax.sharding import PartitionSpec as P

MESH = pl.DeviceIdType.MESH
F32, BF = jnp.float32, jnp.bfloat16
STEPS = 10
GX, GY = 8, 16
R = 144
GR = 3
VMEM = pltpu.VMEM


def band(coefs, delta):
    k, n = np.arange(128)[:, None], np.arange(128)[None, :]
    dx = (k // 32 + 4 * delta) - n // 32
    dz = k % 32 - n % 32
    out = np.zeros((128, 128), np.float32)
    for (a, b), v in coefs.items():
        out[(dx == a) & (dz == b)] = v
    return out


def band_weights():
    c1 = {-2: 1, -1: -8, 1: 8, 2: -1}
    c2 = {-2: -1, -1: 16, 0: -30, 1: 16, 2: -1}
    dx = {(a, 0): v for a, v in c1.items()}
    dz = {(0, a): v for a, v in c1.items()}
    dxx = {(a, 0): v for a, v in c2.items()}
    dzz = {(0, a): v for a, v in c2.items()}
    dxz = {(a, b): v * w for a, v in c1.items() for b, w in c1.items()}
    lap = dict(dxx)
    for key, v in dzz.items():
        lap[key] = lap.get(key, 0) + v
    dxx12 = {key: 12 * v for key, v in dxx.items()}
    dzz12 = {key: 12 * v for key, v in dzz.items()}

    def two(m):
        return np.concatenate([m, m], 0)

    def beside(o):
        return np.where(np.arange(128)[:, None] < 64, band(o, 1), band(o, -1))

    def inner(ops):
        return np.concatenate([two(band(o, 0)) for o in ops], 1)

    def full(ops):
        return np.concatenate([inner(ops), np.concatenate([two(beside(o)) for o in ops], 1)], 0)

    def select(c):
        k, n = np.arange(128)[:, None], np.arange(128)[None, :]
        return two(((k % 32 == 0) & (n % 12 == c * 4 + k // 32) & (n < 120)).astype(np.float32))

    wu = full([lap, dxx12, dxz, dx])
    ww = full([lap, dxz])
    ww0 = inner([dzz12, dz])
    wv = full([lap, dx])
    wv0 = np.concatenate([inner([dz]), select(1)], 1)
    wsel = np.stack([select(0), select(2)])
    k, n = np.arange(128)[:, None], np.arange(128)[None, :]
    wslot = np.stack([two(((n == k // 4 * 4 + s) & (k < 120)).astype(np.float32)) for s in range(4)])
    return [jnp.asarray(a.astype(ml_dtypes.bfloat16)) for a in (wu, ww, ww0, wv, wv0, wsel, wslot)]


def d1(m2, m1, p1, p2):
    return (m2 - p2) + 8.0 * (p1 - m1)


def wave_kernel(
    now_hbm, prev_hbm, shear_hbm, bulk_hbm, found, wu_hbm, ww_hbm, ww0_hbm, wv_hbm, wv0_hbm, wsel_hbm, wslot_hbm,
    out_now, out_prev, out_ground,
    now, prev, shear, bulk, wu, ww, ww0, wv, wv0, wsel, wslot, in_sem, out_sem,
    WA, WB, SB, BH, BHE, MU, HIST, PS, PR, G1, A1, B1, out_rows,
    send_sem, recv_sem, send_y, recv_y, send_x, recv_x,
):
    gx, gy = lax.axis_index("gx"), lax.axis_index("gy")

    def has(dx, dy):
        return (gx + dx >= 0) & (gx + dx < GX) & (gy + dy >= 0) & (gy + dy < GY)

    dirs = [
        (1, 1, 8), (1, -1, 8), (0, 1, 8), (0, -1, 8), (1, 0, 8),
        (-1, 1, 1), (-1, -1, 1), (0, 1, 1), (0, -1, 1), (-1, 0, 1),
        (0, 1, 0), (0, -1, 0),
    ]
    WS = (WA, WB)
    lane = lax.broadcasted_iota(jnp.int32, (64, 128), 1)

    loads = [pltpu.make_async_copy(now_hbm.at[c], now.at[c], in_sem.at[c]) for c in range(3)]
    loads += [pltpu.make_async_copy(prev_hbm.at[c], prev.at[c], in_sem.at[3 + c]) for c in range(3)]
    rest = (
        (shear_hbm, shear), (bulk_hbm, bulk), (wu_hbm, wu), (ww_hbm, ww), (ww0_hbm, ww0),
        (wv_hbm, wv), (wv0_hbm, wv0), (wsel_hbm, wsel), (wslot_hbm, wslot),
    )
    loads += [pltpu.make_async_copy(src, dst, in_sem.at[6 + i]) for i, (src, dst) in enumerate(rest)]
    for load in loads:
        load.start()

    for W in WS:
        for xs in (0, 9):
            W[:, xs] = jnp.zeros((3, R, 128), F32)
        for y in (0, 136):
            W[:, 1:9, y : y + 8, :] = jnp.zeros((3, 8, 8, 128), F32)
    PR[...] = jnp.zeros_like(PR)
    HIST[...] = jnp.zeros_like(HIST)

    barrier = pltpu.get_barrier_semaphore()
    count = (GX - 1) + (GY - 1)
    for i in range(1, GX):
        pl.semaphore_signal(barrier, inc=1, device_id={"gx": (gx + i) % GX, "gy": gy}, device_id_type=MESH)
    for i in range(1, GY):
        pl.semaphore_signal(barrier, inc=1, device_id={"gx": gx, "gy": (gy + i) % GY}, device_id_type=MESH)
    for dx, dy in ((1, 1), (1, -1), (-1, 1), (-1, -1)):
        ok = has(dx, dy)
        count = count + ok.astype(jnp.int32)

        @pl.when(ok)
        def _():
            pl.semaphore_signal(barrier, inc=1, device_id={"gx": gx + dx, "gy": gy + dy}, device_id_type=MESH)

    def turned(read, xs):
        return jnp.concatenate([read(xs * 4 + xl + 256 * q) for xl in range(4) for q in range(4)], 0).T

    def load_field(src, W, c):
        def body(i, _):
            for k in range(4):
                xs = 4 * i + k
                W[c, xs + 1, 8:136, :] = turned(lambda at: src[c, pl.ds(at, 8, stride=32), :], xs)
            return 0

        lax.fori_loop(0, 2, body, 0)

    for c in range(3):
        loads[c].wait()
        load_field(now, WA, c)
    pl.semaphore_wait(barrier, count)

    def copy(p, d):
        dx, dy, slab = dirs[d]
        W = WS[p]
        if dy == 0:
            side = 1 if dx > 0 else 0
            src, dst = PS.at[p, side], PR.at[p, 1 - side]
        else:
            y_src, y_dst = (134, 6) if dy > 0 else (8, 136)
            if dx == 0:
                slabs = pl.ds(slab, 1) if slab else pl.ds(2, 6)
                src, dst = W.at[:, slabs, pl.ds(y_src, 2), :], W.at[:, slabs, pl.ds(y_dst, 2), :]
            else:
                x_src, x_dst = (8, 0) if dx > 0 else (1, 9)
                src, dst = W.at[0:2, x_src, pl.ds(y_src, 2), :], W.at[0:2, x_dst, pl.ds(y_dst, 2), :]
        return pltpu.make_async_remote_copy(
            src_ref=src, dst_ref=dst, send_sem=send_sem.at[p, d], recv_sem=recv_sem.at[p, d],
            device_id={"gx": gx + dx, "gy": gy + dy}, device_id_type=MESH,
        )

    def start(p, slab):
        for d, (dx, dy, after) in enumerate(dirs):
            if after == slab:

                @pl.when(has(dx, dy))
                def _():
                    copy(p, d).start()

    def wait(p, dx_recv, dx_send):
        for d, (dx, dy, _) in enumerate(dirs):
            if dx == dx_recv:

                @pl.when(has(-dx, -dy))
                def _():
                    copy(p, d).wait_recv()

            if dx == dx_send:

                @pl.when(has(dx, dy))
                def _():
                    copy(p, d).wait_send()

    def send_side(p, xs):
        W = WS[p]
        for c in range(3):
            low, high = W[c, xs, 8:72, :], W[c, xs, 72:136, :]
            if xs == 8:
                PS[p, 1, c] = jnp.where(lane < 64, pltpu.roll(low, 64, 1), high)
            else:
                PS[p, 0, c] = jnp.where(lane < 64, low, pltpu.roll(high, 64, 1))
        start(p, xs)

    def halves(x):
        hi = x.astype(BF)
        return hi, (x - hi.astype(F32)).astype(BF)

    def put(B, c, x, own, up, down, n):
        hi, lo = halves(x)
        if own is not None:
            B[c, pl.ds(own, n), 0:128] = hi
            B[c, pl.ds(own, n), 128:256] = lo
        if up is not None:
            B[c, pl.ds(up, n), 320:384] = hi[:, 64:128]
            B[c, pl.ds(up, n), 448:512] = lo[:, 64:128]
        if down is not None:
            B[c, pl.ds(down, n), 256:320] = hi[:, 0:64]
            B[c, pl.ds(down, n), 384:448] = lo[:, 0:64]

    BASE = {8: 768, 1: 912}

    def split_own(W):
        def body(i, _):
            own = pl.multiple_of(i * 128, 128)
            up = pl.multiple_of(i * 128 + 128, 128)
            down = pl.multiple_of(jnp.where(i == 0, BASE[1], i * 128 - 128), 16)
            for c in range(3):
                put(BH, c, W[c, i + 2, 8:136, :], own, up, down, 128)
            return 0

        lax.fori_loop(0, 6, body, 0)
        for c in range(3):
            put(BH, c, W[c, 8, 8:136, :], BASE[8], None, 5 * 128, 128)
            put(BH, c, W[c, 1, 8:136, :], BASE[1], 0, None, 128)

    def edge(W, c, xs):
        return jnp.concatenate([W[c, xs, 0:8, :], W[c, xs, 136:144, :]], 0)

    def split_edges(W):
        for c in range(3):
            for xs in range(1, 9):
                at = (xs - 2) * 16
                cross = c < 2
                put(
                    BHE, c, edge(W, c, xs),
                    at if 2 <= xs <= 7 else None,
                    at + 16 if xs <= 6 and cross else None,
                    at - 16 if xs >= 3 and cross else None,
                    16,
                )

    def split_side(W, xs):
        base = BASE[xs]
        for c in range(3):
            if xs == 1:
                put(BH, c, W[c, 0, 8:136, :], None, base, None, 128)
            else:
                put(BH, c, W[c, 9, 8:136, :], None, None, base, 128)
            put(BH, c, edge(W, c, xs - 1), None, base + 128, None, 16)
            put(BH, c, edge(W, c, xs), base + 128, None, None, 16)
            put(BH, c, edge(W, c, xs + 1), None, None, base + 128, 16)

    dot = functools.partial(jnp.dot, preferred_element_type=F32)

    def matmuls(at, n, store, surf):
        u = dot(BH[0, pl.ds(at, n), :], wu[...])
        w = dot(BH[2, pl.ds(at, n), :], ww[...])
        w0 = dot(BH[2, pl.ds(at, n), 0:256], ww0[...])
        v = dot(BH[1, pl.ds(at, n), :], wv[...])
        v0 = dot(BH[1, pl.ds(at, n), 0:256], wv0[...])
        store(0, u[:, 0:128])
        store(1, v[:, 0:128])
        store(2, w[:, 0:128])
        store(3, u[:, 128:256] + w[:, 128:256])
        store(4, u[:, 256:384] + w0[:, 0:128])
        store(5, u[:, 384:512] + w0[:, 128:256])
        store(6, v[:, 128:256])
        store(7, v0[:, 0:128])
        surf(v0[:, 128:256] + dot(BH[0, pl.ds(at, n), 0:256], wsel[0]) + dot(BH[2, pl.ds(at, n), 0:256], wsel[1]))

    group = lax.broadcasted_iota(jnp.int32, (128, 128), 1) // 12

    def keep_surface(t, xs, a):
        HIST[xs - 1] = jnp.where(group == t, a, HIST[xs - 1])

    def edge_matmuls():
        wdx, wdz = wu[:, 384:512], ww0[:, 128:256]
        e = dot(BHE[0], wdx) + dot(BHE[2, :, 0:256], wdz)
        f = dot(BHE[1], wdx)
        g = dot(BHE[1, :, 0:256], wdz)
        for k, a in ((5, e), (6, f), (7, g)):
            a = a.reshape(6, 16, 128)
            MU[k, 1:7, 0:8, :] = a[:, 0:8]
            MU[k, 1:7, 136:144, :] = a[:, 8:16]

    def update(xs, blocks, W, N):
        j = xs - 1
        D = (-2, -1, 1, 2)
        for yb in blocks:
            r = lambda d: pl.ds(8 + yb * 8 + d, 8)
            sh = SB[0, j, yb * 8 : yb * 8 + 8, :]
            bu = SB[1, j, yb * 8 : yb * 8 + 8, :]
            mix = [
                MU[3, j, r(0), :] + d1(*[MU[6, j, r(d), :] for d in D]),
                d1(*[MU[5, j, r(d), :] for d in D]),
                MU[4, j, r(0), :] + d1(*[MU[7, j, r(d), :] for d in D]),
            ]
            for c in range(3):
                y = [W[c, xs, r(d), :] for d in D]
                mid = W[c, xs, r(0), :]
                dyy = 16.0 * (y[1] + y[2]) - (y[0] + y[3]) - 30.0 * mid
                lap = MU[c, j, r(0), :] + dyy
                b = mix[c] + 12.0 * dyy if c == 1 else mix[c]
                N[c, xs, r(0), :] = (2.0 * mid - N[c, xs, r(0), :]) + (sh * lap + bu * b)

    stores = [pltpu.make_async_copy(now.at[c], out_now.at[c], out_sem.at[c]) for c in range(3)]
    stores += [pltpu.make_async_copy(prev.at[c], out_prev.at[c], out_sem.at[3 + c]) for c in range(3)]

    def store_fields(which, components):
        dst, W = ((now, WA), (prev, WB))[which]
        for c in components:

            def body(i, _):
                for k in range(4):
                    xs = 4 * i + k
                    m = W[c, xs + 1, 8:136, :].T
                    for xl in range(4):
                        for q in range(4):
                            dst[c, pl.ds(xs * 4 + xl + 256 * q, 8, stride=32), :] = m[(xl * 4 + q) * 8 : (xl * 4 + q) * 8 + 8]
                return 0

            lax.fori_loop(0, 2, body, 0)
            stores[3 * which + c].start()

    def substep(p, t, send_after):
        W, N = WS[p], WS[1 - p]
        split_own(W)

        def body(g, _):
            def store(k, a):
                MU[k, pl.ds(g * GR + 1, GR), 8:136, :] = a.reshape(GR, 128, 128)

            def surf(a):
                for i in range(GR):
                    keep_surface(t, g * GR + 2 + i, a[128 * i : 128 * i + 128])

            matmuls(pl.multiple_of(g * (GR * 128), 128), GR * 128, store, surf)
            for i in range(GR):
                update(g * GR + 2 + i, range(1, 15), W, N)
            return 0

        lax.fori_loop(0, 6 // GR, body, 0)
        wait(p, 0, 0)
        split_edges(W)
        edge_matmuls()

        def body_y(i, _):
            update(i + 2, (0, 15), W, N)
            return 0

        lax.fori_loop(0, 6, body_y, 0)

        def when_more(f):
            if send_after is True:
                f()
            else:
                pl.when(send_after)(f)

        when_more(lambda: start(1 - p, 0))

        def side(xs):
            out = 1 if xs == 8 else -1
            wait(p, -out, out)
            for c in range(3):
                if xs == 1:
                    left = PR[p, 0, c]
                    W[c, 0, 8:72, :] = pltpu.roll(left, 64, 1)
                    W[c, 0, 72:136, :] = left
                else:
                    right = PR[p, 1, c]
                    W[c, 9, 8:72, :] = right
                    W[c, 9, 72:136, :] = pltpu.roll(right, 64, 1)
            split_side(W, xs)

            def store(k, a):
                MU[k, xs - 1, 8:136, :] = a[0:128]
                if k >= 5:
                    MU[k, xs - 1, 0:8, :] = a[128:136]
                    MU[k, xs - 1, 136:144, :] = a[136:144]

            matmuls(BASE[xs], 144, store, lambda a: keep_surface(t, xs, a[0:128]))
            update(xs, range(16), W, N)
            when_more(lambda: send_side(1 - p, xs))

        def both(k, _):
            is_high = k == gx % 2

            @pl.when(is_high)
            def _():
                side(8)

            @pl.when(jnp.logical_not(is_high))
            def _():
                side(1)

            return 0

        if p == 1:

            @pl.when(jnp.logical_not(send_after))
            def _():
                store_fields(1, range(3))

        lax.fori_loop(0, 2, both, 0)

    send_side(0, 8)
    send_side(0, 1)
    start(0, 0)

    for c in range(3):
        loads[3 + c].wait()
        load_field(prev, WB, c)
    loads[6].wait()
    loads[7].wait()

    def load_mod(i, _):
        for k in range(2):
            xs = 2 * i + k
            SB[0, xs] = turned(lambda at: shear[pl.ds(at, 8, stride=32), :], xs) * (1.0 / 12.0)
            SB[1, xs] = turned(lambda at: bulk[pl.ds(at, 8, stride=32), :], xs) * (1.0 / 144.0)
        return 0

    lax.fori_loop(0, 4, load_mod, 0)
    for load in loads[8:]:
        load.wait()

    def pair(i, _):
        substep(0, 2 * i - 1, True)
        substep(1, 2 * i, i < STEPS // 2 - 1)
        return 0

    lax.fori_loop(0, STEPS // 2, pair, 0)

    def last(i, _):
        total = jnp.zeros((128, 128), F32)
        for c in range(3):
            w = wv0[:, 128:256] if c == 1 else wsel[c // 2]
            total = total + dot(jnp.concatenate(halves(WA[c, i + 1, 8:136, :]), 1), w)
        keep_surface(STEPS - 1, i + 1, total)
        return 0

    lax.fori_loop(0, 8, last, 0)

    cells = jnp.concatenate([found[...].astype(F32), jnp.zeros((124, 128), F32)], 0).T.astype(jnp.int32)
    rows = jnp.zeros((128, 128), F32)
    wide = lax.broadcasted_iota(jnp.int32, (128, 256), 1)
    narrow = lax.broadcasted_iota(jnp.int32, (128, 128), 1)
    for s in range(4):
        cell = cells[:, s : s + 1]
        row = (cell // 512) * 128 + cell % 128
        quarter = (cell // 128) % 4
        total = jnp.zeros((128, 256), F32)
        for i in range(4):
            pick = (row == wide + 256 * i).astype(F32).astype(BF)
            h = HIST[2 * i : 2 * i + 2].reshape(256, 128)
            total = total + dot(pick, jnp.concatenate(halves(h), 1))
        got = jnp.where(narrow % 4 == quarter, total[:, 0:128] + total[:, 128:256], 0.0)
        rows = rows + dot(jnp.concatenate(halves(got), 1), wslot[s])
    for i in range(GX):
        G1[:, i, :] = rows[GY * i : GY * i + GY]

    def over_y(i):
        to = (gy + i) % GY
        return pltpu.make_async_remote_copy(
            src_ref=G1.at[to], dst_ref=A1.at[gy], send_sem=send_y.at[i], recv_sem=recv_y.at[i],
            device_id={"gx": gx, "gy": to}, device_id_type=MESH,
        )

    def over_x(i):
        to = (gx + i) % GX
        return pltpu.make_async_remote_copy(
            src_ref=B1.at[to], dst_ref=out_rows.at[gx], send_sem=send_x.at[i], recv_sem=recv_x.at[i],
            device_id={"gx": to, "gy": gy}, device_id_type=MESH,
        )

    for i in range(1, GY):
        over_y(i).start()
    A1[gy] = G1[gy]
    store_fields(0, range(2))
    for i in range(1, GY):
        over_y(i).wait()
    for i in range(GX):
        B1[i] = A1[:, i, :]
    for i in range(1, GX):
        over_x(i).start()
    out_rows[gx] = B1[gx]
    store_fields(0, range(2, 3))
    for i in range(1, GX):
        over_x(i).wait()
    out_ground[...] = out_rows[...]
    for store in stores:
        store.wait()


def bridge_kernel(
    received_hbm, support, col, val_hbm, mass, disp, vel, acc, now, before,
    out_disp, out_vel, out_now, out_before,
    val, ground, state, held, received, sem, pass_sem,
):
    arrive = pltpu.make_async_copy(received_hbm, received, pass_sem.at[4])
    arrive.start()
    copies = []
    for node in range(16):
        c = pltpu.make_async_copy(val_hbm.at[node], val.at[:, :, :, node, :], sem.at[node])
        c.start()
        copies.append(c)
    taken = [pltpu.make_async_copy(src, held.at[i], pass_sem.at[i]) for i, src in enumerate((now, before))]
    passed = [pltpu.make_async_copy(held.at[i], dst, pass_sem.at[2 + i]) for i, dst in enumerate((out_now, out_before))]
    rows = jnp.concatenate([support[0:1, :], support[1:2, :]], 1)
    pick = (lax.broadcasted_iota(jnp.int32, (128, 256), 0) == rows // 4).astype(F32).astype(BF)
    arrive.wait()
    flat = received[...].T
    hi = flat.astype(BF)
    lo = (flat - hi.astype(F32)).astype(BF)
    dot = functools.partial(jnp.dot, preferred_element_type=F32)
    found = dot(hi, pick) + dot(lo, pick)
    slot = lax.broadcasted_iota(jnp.int32, (128, 256), 0) % 4 == rows % 4
    ground[...] = jnp.sum(jnp.where(slot, found, 0.0).reshape(32, 4, 256), axis=1, keepdims=True)
    D, V, A = 0, 6, 12
    for d in range(6):
        state[D + d] = disp[d]
        state[V + d] = vel[d]
        state[A + d] = acc[d]
        state[18 + d] = mass[d]
    for c in copies:
        c.wait()
    for c in taken:
        c.start()
    sub = lax.broadcasted_iota(jnp.int32, (16, 128), 0)
    index = [col[:, j, :] for j in range(1, 4)]

    def step(t, _):
        new = [state[D + d] + state[V + d] + 0.5 * state[A + d] for d in range(6)]
        total = list(new)
        for j in range(4):
            for d in range(6):
                if j == 0:
                    v = new[d]
                else:
                    halves = []
                    for h in range(2):
                        ix = index[j - 1][8 * h : 8 * h + 8]
                        at = jnp.bitwise_and(ix, 7)
                        g0 = jnp.take_along_axis(new[d][0:8], at, axis=0)
                        g1 = jnp.take_along_axis(new[d][8:16], at, axis=0)
                        halves.append(jnp.where(ix >= 8, g1, g0))
                    v = jnp.concatenate(halves, 0)
                for e in range(6):
                    total[e] = total[e] + val[e, d, j] * v
        for d in range(6):
            force = -total[d]
            if d < 3:
                g = ground[t * 3 + d]
                force = force + jnp.where(sub == 0, g[:, 0:128], jnp.where(sub == 15, g[:, 128:256], 0.0))
            new_acc = state[18 + d] * force
            state[V + d] = state[V + d] + 0.5 * (state[A + d] + new_acc)
            state[A + d] = new_acc
            state[D + d] = new[d]
        return 0

    lax.fori_loop(0, STEPS // 2, step, 0)
    for i in range(2):
        taken[i].wait()
        passed[i].start()
    lax.fori_loop(STEPS // 2, STEPS, step, 0)
    for d in range(6):
        out_disp[d] = state[D + d]
        out_vel[d] = state[V + d]
    for c in passed:
        c.wait()


def local(
    wave_now, wave_prev, shear_mod, bulk_mod, found_cell, support_row, block_col, block_val,
    mass_inv, bridge_disp, bridge_vel, bridge_acc,
):
    weights = band_weights()
    vm = pl.BlockSpec(memory_space=VMEM)
    hbm = pl.BlockSpec(memory_space=pl.ANY)
    now, before, outgoing = pl.pallas_call(
        wave_kernel,
        out_shape=[
            jax.ShapeDtypeStruct((3, 1024, 128), F32),
            jax.ShapeDtypeStruct((3, 1024, 128), F32),
            jax.ShapeDtypeStruct((GX, GY, 128), F32),
        ],
        in_specs=[hbm] * 4 + [vm] + [hbm] * 7,
        out_specs=[hbm] * 2 + [vm],
        scratch_shapes=[
            VMEM((3, 1024, 128), F32),
            VMEM((3, 1024, 128), F32),
            VMEM((1024, 128), F32),
            VMEM((1024, 128), F32),
            *[VMEM(a.shape, BF) for a in weights],
            pltpu.SemaphoreType.DMA((15,)),
            pltpu.SemaphoreType.DMA((6,)),
            VMEM((3, 10, R, 128), F32),
            VMEM((3, 10, R, 128), F32),
            VMEM((2, 8, 128, 128), F32),
            VMEM((3, 1056, 512), BF),
            VMEM((3, 96, 512), BF),
            VMEM((8, 8, R, 128), F32),
            VMEM((8, 128, 128), F32),
            VMEM((2, 2, 3, 64, 128), F32),
            VMEM((2, 2, 3, 64, 128), F32),
            VMEM((GY, GX, 128), F32),
            VMEM((GY, GX, 128), F32),
            VMEM((GX, GY, 128), F32),
            VMEM((GX, GY, 128), F32),
            pltpu.SemaphoreType.DMA((2, 12)),
            pltpu.SemaphoreType.DMA((2, 12)),
            pltpu.SemaphoreType.DMA((GY,)),
            pltpu.SemaphoreType.DMA((GY,)),
            pltpu.SemaphoreType.DMA((GX,)),
            pltpu.SemaphoreType.DMA((GX,)),
        ],
        compiler_params=pltpu.CompilerParams(
            collective_id=0, has_side_effects=True, vmem_limit_bytes=56 * 2**20
        ),
    )(
        wave_now.reshape(3, 1024, 128), wave_prev.reshape(3, 1024, 128),
        shear_mod.reshape(1024, 128), bulk_mod.reshape(1024, 128),
        found_cell.reshape(128, 4).T, *weights,
    )
    by_dof = lambda a: jnp.transpose(a, (1, 0, 2))
    field = jax.ShapeDtypeStruct((3, 1024, 128), F32)
    deck_disp, deck_vel, now, before = pl.pallas_call(
        bridge_kernel,
        out_shape=[jax.ShapeDtypeStruct((6, 16, 128), F32)] * 2 + [field] * 2,
        in_specs=[hbm] + [vm] * 2 + [hbm] + [vm] * 4 + [hbm] * 2,
        out_specs=[vm] * 2 + [hbm] * 2,
        scratch_shapes=[
            VMEM((6, 6, 4, 16, 128), F32),
            VMEM((32, 1, 256), F32),
            VMEM((24, 16, 128), F32),
            VMEM((2, 3, 1024, 128), F32),
            VMEM((128, 128), F32),
            pltpu.SemaphoreType.DMA((16,)),
            pltpu.SemaphoreType.DMA((5,)),
        ],
        compiler_params=pltpu.CompilerParams(vmem_limit_bytes=52 * 2**20),
    )(
        outgoing.reshape(128, 128), support_row, block_col, jnp.transpose(block_val, (0, 2, 3, 1, 4)),
        by_dof(mass_inv), by_dof(bridge_disp), by_dof(bridge_vel), by_dof(bridge_acc), now, before,
    )
    return now.reshape(3, 32, 32, 128), before.reshape(3, 32, 32, 128), by_dof(deck_disp), by_dof(deck_vel)


def solution(mesh):
    xy = ("gx", "gy")
    in_specs = (
        P(None, None, "gx", "gy"),
        P(None, None, "gx", "gy"),
        P(None, "gx", "gy"),
        P(None, "gx", "gy"),
        P("gx", "gy", None, None),
        P(None, xy),
        P(None, None, xy),
        P(None, None, None, None, xy),
        P(None, None, xy),
        P(None, None, xy),
        P(None, None, xy),
        P(None, None, xy),
    )
    out_specs = (
        P(None, None, "gx", "gy"),
        P(None, None, "gx", "gy"),
        P(None, None, xy),
        P(None, None, xy),
    )
    return jax.shard_map(local, mesh=mesh, in_specs=in_specs, out_specs=out_specs, check_vma=False)
```

```python
import functools

import jax
import jax.numpy as jnp
import ml_dtypes
import numpy as np
from jax import lax
from jax.experimental import pallas as pl
from jax.experimental.pallas import tpu as pltpu
from jax.sharding import PartitionSpec as P

MESH = pl.DeviceIdType.MESH
F32, BF = jnp.float32, jnp.bfloat16
STEPS = 10
GX, GY = 8, 16
R = 144
GR = 3
VMEM = pltpu.VMEM


def band(coefs, delta):
    k, n = np.arange(128)[:, None], np.arange(128)[None, :]
    dx = (k // 32 + 4 * delta) - n // 32
    dz = k % 32 - n % 32
    out = np.zeros((128, 128), np.float32)
    for (a, b), v in coefs.items():
        out[(dx == a) & (dz == b)] = v
    return out


def band_weights():
    c1 = {-2: 1, -1: -8, 1: 8, 2: -1}
    c2 = {-2: -1, -1: 16, 0: -30, 1: 16, 2: -1}
    dx = {(a, 0): v for a, v in c1.items()}
    dz = {(0, a): v for a, v in c1.items()}
    dxx = {(a, 0): v for a, v in c2.items()}
    dzz = {(0, a): v for a, v in c2.items()}
    dxz = {(a, b): v * w for a, v in c1.items() for b, w in c1.items()}
    lap = dict(dxx)
    for key, v in dzz.items():
        lap[key] = lap.get(key, 0) + v
    dxx12 = {key: 12 * v for key, v in dxx.items()}
    dzz12 = {key: 12 * v for key, v in dzz.items()}

    def two(m):
        return np.concatenate([m, m], 0)

    def beside(o):
        return np.where(np.arange(128)[:, None] < 64, band(o, 1), band(o, -1))

    def inner(ops):
        return np.concatenate([two(band(o, 0)) for o in ops], 1)

    def full(ops):
        return np.concatenate([inner(ops), np.concatenate([two(beside(o)) for o in ops], 1)], 0)

    def select(c):
        k, n = np.arange(128)[:, None], np.arange(128)[None, :]
        return two(((k % 32 == 0) & (n % 12 == c * 4 + k // 32) & (n < 120)).astype(np.float32))

    wu = full([lap, dxx12, dxz, dx])
    ww = full([lap, dxz])
    ww0 = inner([dzz12, dz])
    wv = full([lap, dx])
    wv0 = np.concatenate([inner([dz]), select(1)], 1)
    wsel = np.stack([select(0), select(2)])
    k, n = np.arange(128)[:, None], np.arange(128)[None, :]
    wslot = np.stack([two(((n == k // 4 * 4 + s) & (k < 120)).astype(np.float32)) for s in range(4)])
    return [jnp.asarray(a.astype(ml_dtypes.bfloat16)) for a in (wu, ww, ww0, wv, wv0, wsel, wslot)]


def d1(m2, m1, p1, p2):
    return (m2 - p2) + 8.0 * (p1 - m1)


def wave_kernel(
    now_hbm, prev_hbm, shear_hbm, bulk_hbm, found, wu_hbm, ww_hbm, ww0_hbm, wv_hbm, wv0_hbm, wsel_hbm, wslot_hbm,
    out_now, out_prev, out_ground,
    now, prev, shear, bulk, wu, ww, ww0, wv, wv0, wsel, wslot, in_sem, out_sem,
    WA, WB, SB, BH, BHE, MU, HIST, PS, PR, G1, A1, B1, out_rows,
    send_sem, recv_sem, send_y, recv_y, send_x, recv_x,
):
    gx, gy = lax.axis_index("gx"), lax.axis_index("gy")

    def has(dx, dy):
        return (gx + dx >= 0) & (gx + dx < GX) & (gy + dy >= 0) & (gy + dy < GY)

    dirs = [
        (1, 1, 8), (1, -1, 8), (0, 1, 8), (0, -1, 8), (1, 0, 8),
        (-1, 1, 1), (-1, -1, 1), (0, 1, 1), (0, -1, 1), (-1, 0, 1),
        (0, 1, 0), (0, -1, 0),
    ]
    WS = (WA, WB)
    lane = lax.broadcasted_iota(jnp.int32, (64, 128), 1)

    loads = [pltpu.make_async_copy(now_hbm.at[c], now.at[c], in_sem.at[c]) for c in range(3)]
    loads += [pltpu.make_async_copy(prev_hbm.at[c], prev.at[c], in_sem.at[3 + c]) for c in range(3)]
    rest = (
        (shear_hbm, shear), (bulk_hbm, bulk), (wu_hbm, wu), (ww_hbm, ww), (ww0_hbm, ww0),
        (wv_hbm, wv), (wv0_hbm, wv0), (wsel_hbm, wsel), (wslot_hbm, wslot),
    )
    loads += [pltpu.make_async_copy(src, dst, in_sem.at[6 + i]) for i, (src, dst) in enumerate(rest)]
    for load in loads:
        load.start()

    for W in WS:
        for xs in (0, 9):
            W[:, xs] = jnp.zeros((3, R, 128), F32)
        for y in (0, 136):
            W[:, 1:9, y : y + 8, :] = jnp.zeros((3, 8, 8, 128), F32)
    PR[...] = jnp.zeros_like(PR)
    HIST[...] = jnp.zeros_like(HIST)

    barrier = pltpu.get_barrier_semaphore()
    count = (GX - 1) + (GY - 1)
    for i in range(1, GX):
        pl.semaphore_signal(barrier, inc=1, device_id={"gx": (gx + i) % GX, "gy": gy}, device_id_type=MESH)
    for i in range(1, GY):
        pl.semaphore_signal(barrier, inc=1, device_id={"gx": gx, "gy": (gy + i) % GY}, device_id_type=MESH)
    for dx, dy in ((1, 1), (1, -1), (-1, 1), (-1, -1)):
        ok = has(dx, dy)
        count = count + ok.astype(jnp.int32)

        @pl.when(ok)
        def _():
            pl.semaphore_signal(barrier, inc=1, device_id={"gx": gx + dx, "gy": gy + dy}, device_id_type=MESH)

    def turned(read, xs):
        return jnp.concatenate([read(xs * 4 + xl + 256 * q) for xl in range(4) for q in range(4)], 0).T

    def load_field(src, W, c):
        def body(i, _):
            for k in range(4):
                xs = 4 * i + k
                W[c, xs + 1, 8:136, :] = turned(lambda at: src[c, pl.ds(at, 8, stride=32), :], xs)
            return 0

        lax.fori_loop(0, 2, body, 0)

    for c in range(3):
        loads[c].wait()
        load_field(now, WA, c)
    pl.semaphore_wait(barrier, count)

    def copy(p, d):
        dx, dy, slab = dirs[d]
        W = WS[p]
        if dy == 0:
            side = 1 if dx > 0 else 0
            src, dst = PS.at[p, side], PR.at[p, 1 - side]
        else:
            y_src, y_dst = (134, 6) if dy > 0 else (8, 136)
            if dx == 0:
                slabs = pl.ds(slab, 1) if slab else pl.ds(2, 6)
                src, dst = W.at[:, slabs, pl.ds(y_src, 2), :], W.at[:, slabs, pl.ds(y_dst, 2), :]
            else:
                x_src, x_dst = (8, 0) if dx > 0 else (1, 9)
                src, dst = W.at[0:2, x_src, pl.ds(y_src, 2), :], W.at[0:2, x_dst, pl.ds(y_dst, 2), :]
        return pltpu.make_async_remote_copy(
            src_ref=src, dst_ref=dst, send_sem=send_sem.at[p, d], recv_sem=recv_sem.at[p, d],
            device_id={"gx": gx + dx, "gy": gy + dy}, device_id_type=MESH,
        )

    def start(p, slab):
        for d, (dx, dy, after) in enumerate(dirs):
            if after == slab:

                @pl.when(has(dx, dy))
                def _():
                    copy(p, d).start()

    def wait(p, dx_recv, dx_send):
        for d, (dx, dy, _) in enumerate(dirs):
            if dx == dx_recv:

                @pl.when(has(-dx, -dy))
                def _():
                    copy(p, d).wait_recv()

            if dx == dx_send:

                @pl.when(has(dx, dy))
                def _():
                    copy(p, d).wait_send()

    def send_side(p, xs):
        W = WS[p]
        for c in range(3):
            low, high = W[c, xs, 8:72, :], W[c, xs, 72:136, :]
            if xs == 8:
                PS[p, 1, c] = jnp.where(lane < 64, pltpu.roll(low, 64, 1), high)
            else:
                PS[p, 0, c] = jnp.where(lane < 64, low, pltpu.roll(high, 64, 1))
        start(p, xs)

    def halves(x):
        hi = x.astype(BF)
        return hi, (x - hi.astype(F32)).astype(BF)

    def put(B, c, x, own, up, down, n):
        hi, lo = halves(x)
        if own is not None:
            B[c, pl.ds(own, n), 0:128] = hi
            B[c, pl.ds(own, n), 128:256] = lo
        if up is not None:
            B[c, pl.ds(up, n), 320:384] = hi[:, 64:128]
            B[c, pl.ds(up, n), 448:512] = lo[:, 64:128]
        if down is not None:
            B[c, pl.ds(down, n), 256:320] = hi[:, 0:64]
            B[c, pl.ds(down, n), 384:448] = lo[:, 0:64]

    BASE = {8: 768, 1: 912}

    def split_own(W):
        def body(i, _):
            own = pl.multiple_of(i * 128, 128)
            up = pl.multiple_of(i * 128 + 128, 128)
            down = pl.multiple_of(jnp.where(i == 0, BASE[1], i * 128 - 128), 16)
            for c in range(3):
                put(BH, c, W[c, i + 2, 8:136, :], own, up, down, 128)
            return 0

        lax.fori_loop(0, 6, body, 0)
        for c in range(3):
            put(BH, c, W[c, 8, 8:136, :], BASE[8], None, 5 * 128, 128)
            put(BH, c, W[c, 1, 8:136, :], BASE[1], 0, None, 128)

    def edge(W, c, xs):
        return jnp.concatenate([W[c, xs, 0:8, :], W[c, xs, 136:144, :]], 0)

    def split_edges(W):
        for c in range(3):
            for xs in range(1, 9):
                at = (xs - 2) * 16
                cross = c < 2
                put(
                    BHE, c, edge(W, c, xs),
                    at if 2 <= xs <= 7 else None,
                    at + 16 if xs <= 6 and cross else None,
                    at - 16 if xs >= 3 and cross else None,
                    16,
                )

    def split_side_own(W, xs):
        base = BASE[xs] + 128
        for c in range(3):
            put(BH, c, edge(W, c, xs), base, None, None, 16)
            if xs == 1:
                put(BH, c, edge(W, c, 2), None, None, base, 16)
            else:
                put(BH, c, edge(W, c, 7), None, base, None, 16)

    def split_side_halo(W, p, xs):
        base = BASE[xs]
        for c in range(3):
            if xs == 1:
                left = PR[p, 0, c]
                put(BH, c, pltpu.roll(left, 64, 1), None, base, None, 64)
                put(BH, c, left, None, base + 64, None, 64)
                put(BH, c, edge(W, c, 0), None, base + 128, None, 16)
            else:
                right = PR[p, 1, c]
                put(BH, c, right, None, None, base, 64)
                put(BH, c, pltpu.roll(right, 64, 1), None, None, base + 64, 64)
                put(BH, c, edge(W, c, 9), None, None, base + 128, 16)

    dot = functools.partial(jnp.dot, preferred_element_type=F32)

    def matmuls(at, n, store, surf):
        u = dot(BH[0, pl.ds(at, n), :], wu[...])
        w = dot(BH[2, pl.ds(at, n), :], ww[...])
        w0 = dot(BH[2, pl.ds(at, n), 0:256], ww0[...])
        v = dot(BH[1, pl.ds(at, n), :], wv[...])
        v0 = dot(BH[1, pl.ds(at, n), 0:256], wv0[...])
        store(0, u[:, 0:128])
        store(1, v[:, 0:128])
        store(2, w[:, 0:128])
        store(3, u[:, 128:256] + w[:, 128:256])
        store(4, u[:, 256:384] + w0[:, 0:128])
        store(5, u[:, 384:512] + w0[:, 128:256])
        store(6, v[:, 128:256])
        store(7, v0[:, 0:128])
        surf(v0[:, 128:256] + dot(BH[0, pl.ds(at, n), 0:256], wsel[0]) + dot(BH[2, pl.ds(at, n), 0:256], wsel[1]))

    group = lax.broadcasted_iota(jnp.int32, (128, 128), 1) // 12

    def keep_surface(t, xs, a):
        HIST[xs - 1] = jnp.where(group == t, a, HIST[xs - 1])

    def edge_matmuls():
        wdx, wdz = wu[:, 384:512], ww0[:, 128:256]
        e = dot(BHE[0], wdx) + dot(BHE[2, :, 0:256], wdz)
        f = dot(BHE[1], wdx)
        g = dot(BHE[1, :, 0:256], wdz)
        for k, a in ((5, e), (6, f), (7, g)):
            a = a.reshape(6, 16, 128)
            MU[k, 1:7, 0:8, :] = a[:, 0:8]
            MU[k, 1:7, 136:144, :] = a[:, 8:16]

    def update(xs, blocks, W, N):
        j = xs - 1
        D = (-2, -1, 1, 2)
        for yb in blocks:
            r = lambda d: pl.ds(8 + yb * 8 + d, 8)
            sh = SB[0, j, yb * 8 : yb * 8 + 8, :]
            bu = SB[1, j, yb * 8 : yb * 8 + 8, :]
            mix = [
                MU[3, j, r(0), :] + d1(*[MU[6, j, r(d), :] for d in D]),
                d1(*[MU[5, j, r(d), :] for d in D]),
                MU[4, j, r(0), :] + d1(*[MU[7, j, r(d), :] for d in D]),
            ]
            for c in range(3):
                y = [W[c, xs, r(d), :] for d in D]
                mid = W[c, xs, r(0), :]
                dyy = 16.0 * (y[1] + y[2]) - (y[0] + y[3]) - 30.0 * mid
                lap = MU[c, j, r(0), :] + dyy
                b = mix[c] + 12.0 * dyy if c == 1 else mix[c]
                N[c, xs, r(0), :] = (2.0 * mid - N[c, xs, r(0), :]) + (sh * lap + bu * b)

    stores = [pltpu.make_async_copy(now.at[c], out_now.at[c], out_sem.at[c]) for c in range(3)]
    stores += [pltpu.make_async_copy(prev.at[c], out_prev.at[c], out_sem.at[3 + c]) for c in range(3)]

    def store_fields(which, components):
        dst, W = ((now, WA), (prev, WB))[which]
        for c in components:

            def body(i, _):
                for k in range(4):
                    xs = 4 * i + k
                    m = W[c, xs + 1, 8:136, :].T
                    for xl in range(4):
                        for q in range(4):
                            dst[c, pl.ds(xs * 4 + xl + 256 * q, 8, stride=32), :] = m[(xl * 4 + q) * 8 : (xl * 4 + q) * 8 + 8]
                return 0

            lax.fori_loop(0, 2, body, 0)
            stores[3 * which + c].start()

    def substep(p, t, send_after):
        W, N = WS[p], WS[1 - p]
        split_own(W)

        def body(g, _):
            def store(k, a):
                MU[k, pl.ds(g * GR + 1, GR), 8:136, :] = a.reshape(GR, 128, 128)

            def surf(a):
                for i in range(GR):
                    keep_surface(t, g * GR + 2 + i, a[128 * i : 128 * i + 128])

            matmuls(pl.multiple_of(g * (GR * 128), 128), GR * 128, store, surf)
            for i in range(GR):
                update(g * GR + 2 + i, range(1, 15), W, N)
            return 0

        lax.fori_loop(0, 6 // GR, body, 0)
        wait(p, 0, 0)
        split_edges(W)
        edge_matmuls()

        def body_y(i, _):
            update(i + 2, (0, 15), W, N)
            return 0

        lax.fori_loop(0, 6, body_y, 0)

        def when_more(f):
            if send_after is True:
                f()
            else:
                pl.when(send_after)(f)

        when_more(lambda: start(1 - p, 0))

        def side(xs):
            out = 1 if xs == 8 else -1
            split_side_own(W, xs)
            wait(p, -out, out)
            split_side_halo(W, p, xs)

            def store(k, a):
                MU[k, xs - 1, 8:136, :] = a[0:128]
                if k >= 5:
                    MU[k, xs - 1, 0:8, :] = a[128:136]
                    MU[k, xs - 1, 136:144, :] = a[136:144]

            matmuls(BASE[xs], 144, store, lambda a: keep_surface(t, xs, a[0:128]))
            update(xs, range(16), W, N)
            when_more(lambda: send_side(1 - p, xs))

        def both(k, _):
            is_high = k == jnp.where(gx < GX // 2, 1, 0)

            @pl.when(is_high)
            def _():
                side(8)

            @pl.when(jnp.logical_not(is_high))
            def _():
                side(1)

            return 0

        if p == 1:

            @pl.when(jnp.logical_not(send_after))
            def _():
                store_fields(1, range(3))

        lax.fori_loop(0, 2, both, 0)

    send_side(0, 8)
    send_side(0, 1)
    start(0, 0)

    for c in range(3):
        loads[3 + c].wait()
        load_field(prev, WB, c)
    loads[6].wait()
    loads[7].wait()

    def load_mod(i, _):
        for k in range(2):
            xs = 2 * i + k
            SB[0, xs] = turned(lambda at: shear[pl.ds(at, 8, stride=32), :], xs) * (1.0 / 12.0)
            SB[1, xs] = turned(lambda at: bulk[pl.ds(at, 8, stride=32), :], xs) * (1.0 / 144.0)
        return 0

    lax.fori_loop(0, 4, load_mod, 0)
    for load in loads[8:]:
        load.wait()

    def pair(i, _):
        substep(0, 2 * i - 1, True)
        substep(1, 2 * i, i < STEPS // 2 - 1)
        return 0

    lax.fori_loop(0, STEPS // 2, pair, 0)

    def last(i, _):
        total = jnp.zeros((128, 128), F32)
        for c in range(3):
            w = wv0[:, 128:256] if c == 1 else wsel[c // 2]
            total = total + dot(jnp.concatenate(halves(WA[c, i + 1, 8:136, :]), 1), w)
        keep_surface(STEPS - 1, i + 1, total)
        return 0

    lax.fori_loop(0, 8, last, 0)

    cells = jnp.concatenate([found[...].astype(F32), jnp.zeros((124, 128), F32)], 0).T.astype(jnp.int32)
    rows = jnp.zeros((128, 128), F32)
    wide = lax.broadcasted_iota(jnp.int32, (128, 256), 1)
    narrow = lax.broadcasted_iota(jnp.int32, (128, 128), 1)
    for s in range(4):
        cell = cells[:, s : s + 1]
        row = (cell // 512) * 128 + cell % 128
        quarter = (cell // 128) % 4
        total = jnp.zeros((128, 256), F32)
        for i in range(4):
            pick = (row == wide + 256 * i).astype(F32).astype(BF)
            h = HIST[2 * i : 2 * i + 2].reshape(256, 128)
            total = total + dot(pick, jnp.concatenate(halves(h), 1))
        got = jnp.where(narrow % 4 == quarter, total[:, 0:128] + total[:, 128:256], 0.0)
        rows = rows + dot(jnp.concatenate(halves(got), 1), wslot[s])
    for i in range(GX):
        G1[:, i, :] = rows[GY * i : GY * i + GY]

    def over_y(i):
        to = (gy + i) % GY
        return pltpu.make_async_remote_copy(
            src_ref=G1.at[to], dst_ref=A1.at[gy], send_sem=send_y.at[i], recv_sem=recv_y.at[i],
            device_id={"gx": gx, "gy": to}, device_id_type=MESH,
        )

    def over_x(i):
        to = (gx + i) % GX
        return pltpu.make_async_remote_copy(
            src_ref=B1.at[to], dst_ref=out_rows.at[gx], send_sem=send_x.at[i], recv_sem=recv_x.at[i],
            device_id={"gx": to, "gy": gy}, device_id_type=MESH,
        )

    for i in range(1, GY):
        over_y(i).start()
    A1[gy] = G1[gy]
    store_fields(0, range(2))
    for i in range(1, GY):
        over_y(i).wait()
    for i in range(GX):
        B1[i] = A1[:, i, :]
    for i in range(1, GX):
        over_x(i).start()
    out_rows[gx] = B1[gx]
    store_fields(0, range(2, 3))
    for i in range(1, GX):
        over_x(i).wait()
    out_ground[...] = out_rows[...]
    for store in stores:
        store.wait()


def bridge_kernel(
    received, support, col, val_hbm, mass, disp, vel, acc, now, before,
    out_disp, out_vel, out_now, out_before,
    val, ground, state, held, sem, pass_sem,
):
    copies = []
    for node in range(16):
        c = pltpu.make_async_copy(val_hbm.at[node], val.at[:, :, :, node, :], sem.at[node])
        c.start()
        copies.append(c)
    taken = [pltpu.make_async_copy(src, held.at[i], pass_sem.at[i]) for i, src in enumerate((now, before))]
    passed = [pltpu.make_async_copy(held.at[i], dst, pass_sem.at[2 + i]) for i, dst in enumerate((out_now, out_before))]
    rows = jnp.concatenate([support[0:1, :], support[1:2, :]], 1)
    pick = (lax.broadcasted_iota(jnp.int32, (128, 256), 0) == rows // 4).astype(F32).astype(BF)
    flat = received[...].T
    hi = flat.astype(BF)
    lo = (flat - hi.astype(F32)).astype(BF)
    dot = functools.partial(jnp.dot, preferred_element_type=F32)
    found = dot(hi, pick) + dot(lo, pick)
    slot = lax.broadcasted_iota(jnp.int32, (128, 256), 0) % 4 == rows % 4
    ground[...] = jnp.sum(jnp.where(slot, found, 0.0).reshape(32, 4, 256), axis=1, keepdims=True)
    D, V, A = 0, 6, 12
    for d in range(6):
        state[D + d] = disp[d]
        state[V + d] = vel[d]
        state[A + d] = acc[d]
        state[18 + d] = mass[d]
    for c in copies:
        c.wait()
    for c in taken:
        c.start()
    sub = lax.broadcasted_iota(jnp.int32, (16, 128), 0)
    index = [col[:, j, :] for j in range(1, 4)]

    def step(t, _):
        new = [state[D + d] + state[V + d] + 0.5 * state[A + d] for d in range(6)]
        total = list(new)
        for j in range(4):
            for d in range(6):
                if j == 0:
                    v = new[d]
                else:
                    halves = []
                    for h in range(2):
                        ix = index[j - 1][8 * h : 8 * h + 8]
                        at = jnp.bitwise_and(ix, 7)
                        g0 = jnp.take_along_axis(new[d][0:8], at, axis=0)
                        g1 = jnp.take_along_axis(new[d][8:16], at, axis=0)
                        halves.append(jnp.where(ix >= 8, g1, g0))
                    v = jnp.concatenate(halves, 0)
                for e in range(6):
                    total[e] = total[e] + val[e, d, j] * v
        for d in range(6):
            force = -total[d]
            if d < 3:
                g = ground[t * 3 + d]
                force = force + jnp.where(sub == 0, g[:, 0:128], jnp.where(sub == 15, g[:, 128:256], 0.0))
            new_acc = state[18 + d] * force
            state[V + d] = state[V + d] + 0.5 * (state[A + d] + new_acc)
            state[A + d] = new_acc
            state[D + d] = new[d]
        return 0

    lax.fori_loop(0, STEPS // 2, step, 0)
    for i in range(2):
        taken[i].wait()
        passed[i].start()
    lax.fori_loop(STEPS // 2, STEPS, step, 0)
    for d in range(6):
        out_disp[d] = state[D + d]
        out_vel[d] = state[V + d]
    for c in passed:
        c.wait()


def local(
    wave_now, wave_prev, shear_mod, bulk_mod, found_cell, support_row, block_col, block_val,
    mass_inv, bridge_disp, bridge_vel, bridge_acc,
):
    weights = band_weights()
    vm = pl.BlockSpec(memory_space=VMEM)
    hbm = pl.BlockSpec(memory_space=pl.ANY)
    now, before, outgoing = pl.pallas_call(
        wave_kernel,
        out_shape=[
            jax.ShapeDtypeStruct((3, 1024, 128), F32),
            jax.ShapeDtypeStruct((3, 1024, 128), F32),
            jax.ShapeDtypeStruct((GX, GY, 128), F32),
        ],
        in_specs=[hbm] * 4 + [vm] + [hbm] * 7,
        out_specs=[hbm] * 2 + [vm],
        scratch_shapes=[
            VMEM((3, 1024, 128), F32),
            VMEM((3, 1024, 128), F32),
            VMEM((1024, 128), F32),
            VMEM((1024, 128), F32),
            *[VMEM(a.shape, BF) for a in weights],
            pltpu.SemaphoreType.DMA((15,)),
            pltpu.SemaphoreType.DMA((6,)),
            VMEM((3, 10, R, 128), F32),
            VMEM((3, 10, R, 128), F32),
            VMEM((2, 8, 128, 128), F32),
            VMEM((3, 1056, 512), BF),
            VMEM((3, 96, 512), BF),
            VMEM((8, 8, R, 128), F32),
            VMEM((8, 128, 128), F32),
            VMEM((2, 2, 3, 64, 128), F32),
            VMEM((2, 2, 3, 64, 128), F32),
            VMEM((GY, GX, 128), F32),
            VMEM((GY, GX, 128), F32),
            VMEM((GX, GY, 128), F32),
            VMEM((GX, GY, 128), F32),
            pltpu.SemaphoreType.DMA((2, 12)),
            pltpu.SemaphoreType.DMA((2, 12)),
            pltpu.SemaphoreType.DMA((GY,)),
            pltpu.SemaphoreType.DMA((GY,)),
            pltpu.SemaphoreType.DMA((GX,)),
            pltpu.SemaphoreType.DMA((GX,)),
        ],
        compiler_params=pltpu.CompilerParams(
            collective_id=0, has_side_effects=True, vmem_limit_bytes=56 * 2**20
        ),
    )(
        wave_now.reshape(3, 1024, 128), wave_prev.reshape(3, 1024, 128),
        shear_mod.reshape(1024, 128), bulk_mod.reshape(1024, 128),
        found_cell.reshape(128, 4).T, *weights,
    )
    by_dof = lambda a: jnp.transpose(a, (1, 0, 2))
    field = jax.ShapeDtypeStruct((3, 1024, 128), F32)
    deck_disp, deck_vel, now, before = pl.pallas_call(
        bridge_kernel,
        out_shape=[jax.ShapeDtypeStruct((6, 16, 128), F32)] * 2 + [field] * 2,
        in_specs=[vm] * 3 + [hbm] + [vm] * 4 + [hbm] * 2,
        out_specs=[vm] * 2 + [hbm] * 2,
        scratch_shapes=[
            VMEM((6, 6, 4, 16, 128), F32),
            VMEM((32, 1, 256), F32),
            VMEM((24, 16, 128), F32),
            VMEM((2, 3, 1024, 128), F32),
            pltpu.SemaphoreType.DMA((16,)),
            pltpu.SemaphoreType.DMA((4,)),
        ],
        compiler_params=pltpu.CompilerParams(vmem_limit_bytes=52 * 2**20),
    )(
        outgoing.reshape(128, 128), support_row, block_col, jnp.transpose(block_val, (0, 2, 3, 1, 4)),
        by_dof(mass_inv), by_dof(bridge_disp), by_dof(bridge_vel), by_dof(bridge_acc), now, before,
    )
    return now.reshape(3, 32, 32, 128), before.reshape(3, 32, 32, 128), by_dof(deck_disp), by_dof(deck_vel)


def solution(mesh):
    xy = ("gx", "gy")
    in_specs = (
        P(None, None, "gx", "gy"),
        P(None, None, "gx", "gy"),
        P(None, "gx", "gy"),
        P(None, "gx", "gy"),
        P("gx", "gy", None, None),
        P(None, xy),
        P(None, None, xy),
        P(None, None, None, None, xy),
        P(None, None, xy),
        P(None, None, xy),
        P(None, None, xy),
        P(None, None, xy),
    )
    out_specs = (
        P(None, None, "gx", "gy"),
        P(None, None, "gx", "gy"),
        P(None, None, xy),
        P(None, None, xy),
    )
    return jax.shard_map(local, mesh=mesh, in_specs=in_specs, out_specs=out_specs, check_vma=False)
```
